32 devices in a mesh: emb: 16 (over z, y, core), seq: 2 (over x).
Axes of the slice: x: 2, y: 2, z: 4, core: 2. Of those that a mesh axis runs over, the one named last changes fastest.
Arguments:
- table: bfloat16 [8192, 256], P('emb'), may hold values from -6 to 6
- owner: int32 [64, 512, 1], P(('emb', 'seq')), may hold values from 0 to 15; in each aligned block of 512 rows (0 to 511, 512 to 1023, ..., all dimensions but the last counted through in order) at most 64 rows name the same one
- row: int32 [64, 512], P(('emb', 'seq')), may hold values from 0 to 511
- conv_weight: float32 [4, 768, 256], replicated, may hold values from -0.21875 to 0.21875
- gain: float32 [4, 256], replicated, may hold values from 0.1 to 1.9
- upstream: bfloat16 [64, 512, 256], P(('emb', 'seq')), may hold values from -6 to 6
Outputs:
- weight_grad: float32 [4, 768, 256], replicated
- gain_grad: float32 [4, 256], replicated
- table_grad: float32 [8192, 256], P('emb')
The draws below stay inside these ranges and needn't reach their ends.
Inputs may be any that keep to these rules, and one draw needn't show every extreme that they name: Within the positions of one micro-batch on one device (aligned blocks of 512 positions, in sequence order), at most 64 have the same owner.
All inputs are finite; a program needn't handle non-finite values.
Results may differ from the reference program's by a relative error of at most 0.022.
Values may be sent and summed in bfloat16 or wider, within the bound.
No kernel may reach another device: no remote copies, remote signals or barrier semaphores. Data moves between devices by JAX's collectives and lax.ppermute only.
A program may use at most 64 MiB of HBM per device.

```python
import math
import jax
import jax.numpy as jnp
import numpy as np
from jax import lax

D = 256
KW = 3
LAYERS = 4
L = 512
MB = 2
SEQ_MB = 1
ROWS_DEV = 512
CAP = 64
SEQS = 64
ROWS = 8192
TOKENS = 32768
N_EMB = 16
N_SEQ = 2


def place_ends(values, rng, smallest, high):
    spot = [jax.random.randint(jax.random.fold_in(rng, axis), (), 0, length) for axis, length in enumerate(values.shape)]
    widest = values.shape.index(max(values.shape))
    next_to = spot[:widest] + [(spot[widest] + 1) % values.shape[widest]] + spot[widest + 1:]
    return values.at[tuple(spot)].set(smallest).at[tuple(next_to)].set(high)


def shard_levels(rng, extent, shards, low, high):
    level, own = 1.0, jax.random.fold_in(rng, 6)
    for dim, parts in shards:
        draws = jnp.exp(jax.random.uniform(jax.random.fold_in(own, dim), (parts,), jnp.float32, low / len(shards), high / len(shards)))
        level = level * jnp.repeat(draws, extent[dim] // parts).reshape([-1 if axis == dim else 1 for axis in range(len(extent))])
    return level


def cumulative_ranks(amount, skew):
    loads = [(1 << 20) // math.isqrt(standing ** skew) + 1 for standing in range(1, amount + 1)]
    deviation = 1 + sum(loads) // (1 << 30)
    return np.cumsum(np.array([max(1, weight // deviation) for weight in loads]))


def skewed_ids(own_key, dims, amount, skew):
    grid = cumulative_ranks(amount, skew)
    ticket = jax.random.randint(jax.random.fold_in(own_key, 1), dims, 0, int(grid[amount - 1]))
    rank = jnp.searchsorted(jnp.asarray(grid, jnp.int32), ticket, side="right")
    return jax.random.permutation(jax.random.fold_in(own_key, 2), amount)[rank].astype(jnp.int32)


def shared_out(stream_key, own, number, rows, count, top, bound, skew):
    ranking = jax.random.permutation(stream_key, count)
    crowded, usual = load_shares(count, rows * top, bound, skew, True), load_shares(count, rows * top, bound, skew, False)
    places = jnp.arange(count)

    def named(sizes, offset_by):
        used = int((sizes > 0).sum())
        fixed = max(1, used // 4)
        passed = fixed + (places - fixed + offset_by * (used - fixed)) % max(1, count - fixed)
        return jnp.zeros((count,), jnp.int32).at[ranking[jnp.where(places < fixed, places, passed)]].set(jnp.asarray(sizes, jnp.int32))

    sizes = jnp.where(number % 4 == 0, named(crowded, number // 4), named(usual, number - number // 4 - 1))
    mixed = jax.random.permutation(jax.random.fold_in(own, 3), count)
    giver, sink = mixed[0:count // 2 * 2:2], mixed[1:count // 2 * 2:2]
    slack = jnp.minimum(sizes[giver] - 1, bound - sizes[sink]) // 2
    slack = jnp.where((giver == ranking[0]) | (sink == ranking[0]) | (sizes[sink] == 0), 0, jnp.maximum(slack, 0))
    passed = jax.random.randint(jax.random.fold_in(own, 4), (count // 2,), 0, 1 << 20) % (slack + 1)
    sizes = sizes.at[giver].add(-passed).at[sink].add(passed)
    labels = jnp.searchsorted(jnp.cumsum(sizes), jnp.arange(rows * top), side="right").astype(jnp.int32)
    table = labels.reshape(top, rows).T
    table = table[jax.random.permutation(jax.random.fold_in(own, 1), rows)]
    offset_by = jax.random.randint(jax.random.fold_in(own, 2), (rows, 1), 0, top)
    return jnp.take_along_axis(table, (jnp.arange(top)[None, :] + offset_by) % top, axis=1)


def load_shares(number_of, total, reach, skew, full):
    loads = [(1 << 20) // math.isqrt(standing ** skew) + 1 for standing in range(1, number_of + 1)]
    largest = reach if full else min(reach, max(-(-total // number_of), total * loads[0] // sum(loads)))
    least = 1 if total - largest >= number_of - 1 else 0
    counts, rest = [largest] + [least] * (number_of - 1), total - largest - least * (number_of - 1)
    while rest > 0:
        movable = [i for i in range(1, number_of) if counts[i] < largest] or [i for i in range(1, number_of) if counts[i] < reach]
        mass, budget = sum([loads[i] for i in movable]), rest
        for i in movable:
            more = min(reach - counts[i], max(1, budget * loads[i] // mass), rest)
            counts[i] = counts[i] + more
            rest = rest - more
    return np.array(counts)


def normal_values(key, dims, deviation, reach, cuts=(), held_as=jnp.bfloat16):
    values = jax.random.normal(key, dims, jnp.float32) * deviation
    if len(cuts) > 0:
        values = shard_levels(key, dims, cuts, -0.22, 0.18) * values
    return jnp.clip(values, min=-reach, max=reach).astype(held_as)


def setup_inputs(seed: int = 0) -> dict:
    splits = jax.random.split(jax.random.key(seed), 7)
    table = normal_values(splits[0], (ROWS, D), 1.0, 6.0, ((0, 16),))
    owner_keys = jax.random.split(jax.random.fold_in(splits[1], 1), SEQS * L // (SEQ_MB * L))
    owner_turns = jax.random.permutation(jax.random.fold_in(splits[1], 3), SEQS * L // (SEQ_MB * L))
    owner = jax.vmap(lambda own, number: shared_out(jax.random.fold_in(splits[1], 2), own, number, SEQ_MB * L, N_EMB, 1, CAP, 2))(owner_keys, owner_turns).reshape((SEQS, L, 1))
    row = place_ends(skewed_ids(splits[2], (SEQS, L), ROWS_DEV, 1), jax.random.fold_in(splits[2], 3), 0, ROWS_DEV - 1).astype(jnp.int32)
    conv_weight = normal_values(splits[3], (LAYERS, KW * D, D), (KW * D) ** -0.5, 0.21875, (), jnp.float32)
    gain = jnp.clip(1.0 + 0.18 * jax.random.normal(splits[4], (LAYERS, D), jnp.float32), 0.1, 1.9)
    upstream = normal_values(splits[5], (SEQS, L, D), 1.0, 6.0, ((0, 32),))
    return dict(table=table, owner=owner, row=row, conv_weight=conv_weight, gain=gain, upstream=upstream)


def shift_back(values, steps):
    return jnp.pad(values, ((0, 0), (steps, 0), (0, 0)))[:, :values.shape[1]]

def shift_ahead(values, steps):
    return jnp.pad(values, ((0, 0), (0, steps), (0, 0)))[:, steps:]

def gelu_tanh(values):
    return jax.nn.gelu(values, approximate=True)

def forward_block(state, weight, gain_row, dilation):
    width = state.shape[-1]
    statef = state.astype(jnp.float32)
    centred = statef - lax.optimization_barrier(jnp.mean(statef, axis=-1, keepdims=True))
    inverse = lax.rsqrt(lax.optimization_barrier(jnp.mean(centred * centred, axis=-1, keepdims=True)) + 1e-05)
    normed = centred * inverse
    hidden = (normed * gain_row).astype(jnp.bfloat16)
    stacked = jnp.concatenate([hidden, shift_back(hidden, dilation), shift_back(hidden, 2 * dilation)], axis=-1)
    flat = stacked.reshape(-1, 3 * width)
    conv = jnp.dot(flat, weight.astype(jnp.bfloat16), preferred_element_type=jnp.float32).reshape(state.shape)
    result = (statef + gelu_tanh(conv)).astype(jnp.bfloat16)
    return (result, (flat, normed, inverse, conv))

def backward_block(cotangent, saved, weight, gain_row, dilation):
    flat, normed, inverse, conv = saved
    width = cotangent.shape[-1]
    slope = jax.jvp(gelu_tanh, (conv,), (jnp.ones_like(conv),))[1]
    cotf = cotangent.astype(jnp.float32)
    dconv = (cotf * slope).astype(jnp.bfloat16).reshape(-1, width)
    dweight = lax.dot_general(flat, dconv, (((0,), (0,)), ((), ())), preferred_element_type=jnp.float32)
    dflat = jnp.dot(dconv, weight.astype(jnp.bfloat16).T, preferred_element_type=jnp.float32)
    dflat = dflat.reshape(cotangent.shape[:-1] + (3 * width,))
    dhidden = dflat[..., :width] + shift_ahead(dflat[..., width:2 * width], dilation)
    dhidden = dhidden + shift_ahead(dflat[..., 2 * width:], 2 * dilation)
    dgain = lax.optimization_barrier(jnp.sum(dhidden * normed, axis=(0, 1)))
    dnorm = dhidden * gain_row
    dstate = inverse * (dnorm - lax.optimization_barrier(jnp.mean(dnorm, axis=-1, keepdims=True)) - normed * lax.optimization_barrier(jnp.mean(dnorm * normed, axis=-1, keepdims=True)))
    return ((cotf + dstate).astype(jnp.bfloat16), dweight, dgain)

def run_stack(embed, weights, gains, cotangent):
    state = embed
    saves = []
    for layer in range(weights.shape[0]):
        state, saved = forward_block(state, weights[layer], gains[layer], 2 ** layer)
        saves.append(saved)
    weight_parts = []
    gain_parts = []
    for layer in reversed(range(weights.shape[0])):
        cotangent, dweight, dgain = backward_block(cotangent, saves[layer], weights[layer], gains[layer], 2 ** layer)
        weight_parts.insert(0, dweight)
        gain_parts.insert(0, dgain)
    return (cotangent, jnp.stack(weight_parts), jnp.stack(gain_parts))

def reference(table, owner, row, conv_weight, gain, upstream):
    ids = (owner[:, :, 0] * ROWS_DEV + row).astype(jnp.int32)
    embed = table[ids]
    group = MB * SEQ_MB * N_SEQ
    blocks = SEQS // group

    def one(pair):
        return run_stack(pair[0], conv_weight, gain, pair[1])
    d_embed, weight_parts, gain_parts = lax.map(one, (embed.reshape(blocks, group, L, D), upstream.reshape(blocks, group, L, D)))
    scale = float(TOKENS) ** (-0.5)
    weight_grad = lax.optimization_barrier(jnp.sum(weight_parts, axis=0)) * scale
    gain_grad = lax.optimization_barrier(jnp.sum(gain_parts, axis=0)) * scale
    table_grad = jnp.zeros((ROWS, D), jnp.float32).at[ids.reshape(-1)].add(d_embed.reshape(-1, D).astype(jnp.float32))
    return (weight_grad, gain_grad, table_grad)
```

```python
import functools
import math

import jax
import jax.numpy as jnp
from jax import lax
from jax.experimental import pallas as pl
from jax.experimental.pallas import tpu as pltpu
from jax.sharding import PartitionSpec as P

MB = 2
TILE = 128
CHUNK = 256
PAD = 16
GROUP = 16
F32 = jnp.float32
BF16 = jnp.bfloat16
VMEM = pl.BlockSpec(memory_space=pltpu.VMEM)
SMEM = pl.BlockSpec(memory_space=pltpu.SMEM)
ANY = pl.BlockSpec(memory_space=pl.ANY)


def iota(shape, axis):
    return lax.broadcasted_iota(jnp.int32, shape, axis)


def one_hot(mask):
    return jnp.where(mask, 1.0, 0.0).astype(BF16)


def dot(a, b, contract=(1, 0)):
    return lax.dot_general(
        a, b, (((contract[0],), (contract[1],)), ((), ())), preferred_element_type=F32
    )


def log2(number):
    return int(number).bit_length() - 1


def ordered(near):
    top = near // 2
    steps = sorted(range(1, near), key=lambda step: (step < 2, step & 1, step < top, step < top + 2))
    return [0] + steps


def returning(chips):
    return [0] + sorted(range(1, chips), key=lambda step: (step & 1, step))


def params(mib):
    return pltpu.CompilerParams(vmem_limit_bytes=mib * 2**20)


def request_kernel(
    slab, place_ref, ids_ref, table_hbm, request_ref, code_ref, table_ref, sem
):
    copy = pltpu.make_async_copy(table_hbm, table_ref, sem)
    copy.start()
    near = request_ref.shape[0]
    reach = request_ref.shape[1] // 2
    batches, count = ids_ref.shape
    capacity = reach // batches
    upper = one_hot(iota((count, count), 0) <= iota((count, count), 1))
    for batch in range(batches):
        ids = ids_ref[batch : batch + 1, :]
        owners, rows = ids >> log2(slab), ids & (slab - 1)
        peers = owners & (near - 1)
        sides = (owners >> log2(near)) ^ place_ref[3]
        marks = jnp.where(iota((2 * near, count), 0) == sides * near + peers, 1.0, 0.0)
        ranks = dot(marks.astype(BF16), upper)
        slots = (jnp.sum(marks * ranks, axis=0, keepdims=True) - 1.0).astype(jnp.int32)
        code_ref[batch : batch + 1, :] = ((peers ^ place_ref[5]) * 2 + sides) * capacity + slots
        spots = one_hot(iota((capacity, count), 0) == slots)
        high = (marks * (rows >> 8).astype(F32)).astype(BF16)
        low = (marks * (rows & 255).astype(F32)).astype(BF16)
        asked = dot(high, spots, (1, 1)) * 256.0 + dot(low, spots, (1, 1))
        for side in range(2):
            start = side * reach + batch * capacity
            request_ref[:, start : start + capacity] = asked[
                side * near : (side + 1) * near
            ].astype(jnp.int32)
    copy.wait()


def near_kernel(place_ref, asked_ref, table_ref, turned_ref, *served_refs):
    near, both = asked_ref.shape
    reach = both // 2
    slab = table_ref.shape[0]
    asked = jnp.concatenate(
        [asked_ref[pl.ds(place_ref[5] ^ step, 1), :] for step in range(near)], axis=0
    )
    turned_ref[...] = asked
    columns = jnp.transpose(asked.astype(F32)).astype(jnp.int32)
    for step, served_ref in enumerate(served_refs):
        picks = one_hot(columns[:reach, step : step + 1] == iota((reach, slab), 1))
        served_ref[...] = dot(picks, table_ref[...]).astype(BF16)


def far_kernel(asked_ref, table_ref, *refs):
    near, both = asked_ref.shape
    reach = both // 2
    slab = table_ref.shape[0]
    columns = jnp.transpose(asked_ref[...].astype(F32)).astype(jnp.int32)
    for step in range(near):
        picks = one_hot(columns[reach:, step : step + 1] == iota((reach, slab), 1))
        refs[near + step][:reach, :] = refs[step][...]
        refs[near + step][reach:, :] = dot(picks, table_ref[...]).astype(BF16)


def collect_kernel(place_ref, asked_ref, after_ref, *refs):
    del after_ref
    near, both = asked_ref.shape
    reach = both // 2
    order = returning(near // 2)
    returned, refs = [refs[order.index(chip)] for chip in range(near // 2)], refs[near // 2 :]
    keeps, messages, parts_s = refs[:2], refs[2:-1], refs[-1]
    slab = parts_s.shape[1]
    share = slab // (1 + len(messages))
    for side in range(2):
        span = slice(side * reach, (side + 1) * reach)
        picks = [
            one_hot(iota((slab, reach), 0) == asked_ref[peer : peer + 1, span])
            for peer in range(near)
        ]
        rows = [ref[core, span, :] for ref in returned for core in range(2)]
        total = None
        pair = 2 if reach % 128 == 0 else 1
        for spot in range(0, near, pair):
            term = dot(
                jnp.concatenate(picks[spot : spot + pair], axis=1),
                jnp.concatenate(rows[spot : spot + pair], axis=0),
            )
            total = term if total is None else total + term
        parts_s[side] = total
        for step in range(1 + len(messages)):
            spot = pl.multiple_of((place_ref[4] ^ step) * share, share)
            value = parts_s[side, pl.ds(spot, share), :]
            if step == 0:
                keeps[side][...] = value
            else:
                messages[step - 1][side * share : (side + 1) * share, :] = value.astype(BF16)


def gain_block(values):
    high = values.astype(BF16)
    low = (values - high.astype(F32)).astype(BF16)
    rest = GROUP - 2 * values.shape[0]
    return jnp.concatenate([high, low, jnp.zeros((rest, values.shape[1]), BF16)], axis=0)


def gain_values(block, layers):
    blockf = block.astype(F32)
    return blockf[:layers] + blockf[layers : 2 * layers]


def stack_kernel(
    place_ref, column_ref, weight_ref, gain_hbm, upstream_hbm, *refs,
):
    arrived_refs, refs = refs[:-18], refs[-18:]
    gain_ref, upstream_ref, sems = refs[15:]
    copies = [
        pltpu.make_async_copy(gain_hbm, gain_ref, sems.at[0]),
        pltpu.make_async_copy(upstream_hbm, upstream_ref, sems.at[1]),
    ]
    for copy in copies:
        copy.start()
    order = ordered(len(arrived_refs))
    fetched_refs = [arrived_refs[order.index(step)] for step in range(len(order))]
    g_ref, keep_ref, sent_ref, block_ref = refs[:4]
    x_s, h_s, hidden_s, normed_s, inverse_s, slope_s, dconv_s, spread_s, dw_s = refs[4:13]
    rounded_s, turned_s = refs[13:15]
    layers, taps, width = weight_ref.shape
    shards, reach = 2 * len(fetched_refs), fetched_refs[0].shape[0] // 2
    tokens = column_ref.shape[0]
    batches = MB
    length = tokens // batches
    capacity = reach // batches
    wide = shards * capacity
    per = length // CHUNK
    steps = taps // width

    def at(seq, j):
        return pl.ds(seq * length + j * CHUNK, CHUNK)

    def inside(seq, j, ahead, size=CHUNK):
        return pl.ds(seq * (length + PAD) + j * CHUNK + ahead, size)

    for batch in range(batches):
        start = batch * (length + PAD)
        for side in range(2):
            h_s[side, start : start + PAD, :] = jnp.zeros((PAD, width), F32)
            dconv_s[side, start + length : start + length + PAD, :] = jnp.zeros((PAD, width), F32)
    dw_s[...] = jnp.zeros(dw_s.shape, F32)
    for layer in range(layers):
        for start in range(0, taps, width):
            value = weight_ref[layer, start : start + width, :]
            rounded_s[layer, start : start + width, :] = value.astype(BF16)
            turned_s[layer, start : start + width, :] = jnp.transpose(value).astype(BF16)

    copies[0].wait()

    def normalise(seq, j, layer, value):
        centred = value - jnp.mean(value, axis=-1, keepdims=True)
        inverse = lax.rsqrt(jnp.mean(centred * centred, axis=-1, keepdims=True) + 1e-05)
        normed = centred * inverse
        normed_s[layer, at(seq, j), :] = normed
        inverse_s[layer, at(seq, j), :] = jnp.broadcast_to(inverse, (CHUNK, 128))
        hidden = normed * gain_ref[layer : layer + 1, :]
        h_s[layer % 2, inside(seq, j, PAD), :] = hidden
        hidden_s[layer, at(seq, j), :] = hidden.astype(BF16)

    for batch in range(batches):
        held = jnp.concatenate(
            [
                ref[side * reach + batch * capacity : side * reach + (batch + 1) * capacity, :]
                for ref in fetched_refs
                for side in range(2)
            ],
            axis=0,
        )
        for j in range(per):
            picks = one_hot(column_ref[at(batch, j), :] == iota((CHUNK, wide), 1))
            value = dot(picks, held)
            x_s[at(batch, j), :] = value
            normalise(batch, j, 0, value)

    root = math.sqrt(2.0 / math.pi)
    for layer in range(layers):
        dilation = 2**layer

        for seq in range(batches):
            for j in range(per):
                view = h_s[layer % 2, inside(seq, j, 0, CHUNK + PAD), :]
                stacked = jnp.concatenate(
                    [
                        view[PAD - tap * dilation : PAD - tap * dilation + CHUNK].astype(BF16)
                        for tap in range(steps)
                    ],
                    axis=1,
                )
                conv = dot(stacked, rounded_s[layer])
                square = conv * conv
                curve = jnp.tanh(conv * (root + (0.044715 * root) * square))
                half = 0.5 + 0.5 * curve
                gelu = conv * half
                slope_s[layer, at(seq, j), :] = half + gelu * (1.0 - curve) * (
                    root + (3.0 * 0.044715 * root) * square
                )
                if layer + 1 < layers:
                    value = (x_s[at(seq, j), :] + gelu).astype(BF16).astype(F32)
                    x_s[at(seq, j), :] = value
                    normalise(seq, j, layer + 1, value)

    def weigh(seq, layer):
        whole = pl.ds(seq * length, length)
        term = dot(hidden_s[layer, whole, :], spread_s[layer % 2, whole, :], (0, 0))
        for tap in range(steps):
            rows = pl.ds(layer * taps + tap * width, width)
            dw_s[rows, :] += term[:, tap * width : (tap + 1) * width]

    copies[1].wait()
    for seq in range(batches):
        for j in range(per):
            cotangent = upstream_ref[at(seq, j), :].astype(F32)
            dconv = (cotangent * slope_s[layers - 1, at(seq, j), :]).astype(BF16).astype(F32)
            dconv_s[(layers - 1) % 2, inside(seq, j, 0), :] = dconv

    gains = [None] * layers
    for layer in reversed(range(layers)):
        dilation = 2**layer

        total = jnp.zeros((8, width), F32)
        for seq in range(batches):
            if layer + 1 < layers:
                weigh(seq, layer + 1)
            for j in range(per):
                view = dconv_s[layer % 2, inside(seq, j, 0, CHUNK + PAD), :]
                spread = jnp.concatenate(
                    [
                        view[tap * dilation : tap * dilation + CHUNK].astype(BF16)
                        for tap in range(steps)
                    ],
                    axis=1,
                )
                spread_s[layer % 2, at(seq, j), :] = spread
                dhidden = dot(spread, turned_s[layer])
                normed = normed_s[layer, at(seq, j), :]
                product = dhidden * normed
                gain_row = gain_ref[layer : layer + 1, :]
                dnorm = dhidden * gain_row
                middle = jnp.mean(dnorm, axis=-1, keepdims=True)
                along = jnp.mean(product * gain_row, axis=-1, keepdims=True)
                inverse = inverse_s[layer, at(seq, j), :]
                inverse = jnp.concatenate([inverse] * (width // 128), axis=1)
                held = upstream_ref if layer == layers - 1 else g_ref
                cotangent = held[at(seq, j), :].astype(F32) + inverse * (
                    dnorm - middle - normed * along
                )
                cotangent = cotangent.astype(BF16)
                g_ref[at(seq, j), :] = cotangent
                if layer > 0:
                    dconv = cotangent.astype(F32) * slope_s[layer - 1, at(seq, j), :]
                    dconv_s[(layer - 1) % 2, inside(seq, j, 0), :] = dconv.astype(BF16).astype(F32)
                total = total + jnp.sum(product.reshape(CHUNK // 8, 8, width), axis=0)
        gains[layer] = jnp.sum(total, axis=0, keepdims=True)

    for batch in range(batches):
        weigh(batch, 0)
    half = keep_ref.shape[0]
    mine = place_ref[0]
    keep_ref[...] = dw_s[pl.ds(pl.multiple_of(mine * half, half), half), :].astype(BF16)
    sent_ref[:half, :] = dw_s[pl.ds(pl.multiple_of((1 - mine) * half, half), half), :].astype(BF16)
    block = gain_block(jnp.concatenate(gains, axis=0))
    sent_ref[half:, :] = block
    block_ref[...] = block


def place_kernel(code_ref, value_ref, *outgoing_refs):
    chips = outgoing_refs[0].shape[0]
    reach = outgoing_refs[0].shape[1] // 2
    batches, length = code_ref.shape
    capacity = reach // batches
    span = TILE // capacity
    for batch in range(batches):
        codes = code_ref[batch : batch + 1, :]
        whole = value_ref[batch * length : (batch + 1) * length, :]
        for j in range(4 * chips // span):
            picks = one_hot(iota((TILE, length), 0) + j * TILE == codes)
            rows = dot(picks, whole).astype(BF16)
            for spot in range(span):
                peer, side = divmod(j * span + spot, 2)
                start = side * reach + batch * capacity
                outgoing_refs[peer % 2][peer // 2, start : start + capacity, :] = rows[
                    spot * capacity : (spot + 1) * capacity
                ]


def pack_kernel(same_ref, other_ref, after_ref, *packed_refs):
    del after_ref
    for chip, ref in enumerate(packed_refs):
        ref[0] = same_ref[chip]
        ref[1] = other_ref[chip]


def tree(values):
    values = list(values)
    while len(values) > 1:
        values = [values[i] + values[i + 1] for i in range(0, len(values), 2)]
    return values[0]


def fold_kernel(layers, arrived, parts, spot, place_ref, keep_ref, block_ref, *refs):
    messages, outs = refs[:arrived], refs[-1 - parts :]
    size = keep_ref.shape[0]
    block = tree(
        [gain_values(block_ref[...], layers)]
        + [gain_values(message[size:, :], layers) for message in messages]
    )
    block = gain_block(block)
    piece = size // parts
    mine = place_ref[spot]
    for part in range(parts):
        rows = pl.ds(pl.multiple_of((mine ^ part) * piece, piece), piece)
        value = tree([keep_ref[rows, :].astype(F32)] + [m[rows, :].astype(F32) for m in messages])
        if part == 0:
            outs[0][...] = value
        else:
            outs[1 + part][:piece, :] = value.astype(BF16)
            outs[1 + part][piece:, :] = block
    outs[1][...] = block


def last_kernel(layers, scale, keep_ref, block_ref, *refs):
    messages, outs = refs[:-2], refs[-2:]
    size = keep_ref.shape[0]
    outs[0][...] = tree([keep_ref[...]] + [m[:size, :].astype(F32) for m in messages]).astype(BF16)
    block = tree(
        [gain_values(block_ref[...], layers)]
        + [gain_values(message[size:, :], layers) for message in messages]
    )
    outs[1][...] = block * scale


def finish_kernel(line, scale, side, place_ref, *refs):
    rows_s, sems = refs[-2:]
    out_ref = refs[-3 - side]
    square, block, _ = rows_s.shape
    piece = block // line
    copies = []
    for outer, ref in enumerate(refs[:square]):
        for inner in range(line):
            target = pl.multiple_of((place_ref[2] ^ inner) * piece, piece)
            rows_s[outer, pl.ds(target, piece), :] = (
                ref[inner * piece : (inner + 1) * piece, :].astype(F32) * scale
            )
        spot = (place_ref[0] ^ side) * square + (place_ref[1] ^ outer)
        rows = pl.ds(pl.multiple_of(spot * block, block), block)
        copies.append(pltpu.make_async_copy(rows_s.at[outer], out_ref.at[rows, :], sems.at[outer]))
        copies[-1].start()
    if side == 1:
        refs[-3][...] = jnp.zeros(refs[-3].shape, F32)
    for copy in copies:
        copy.wait()


def line_kernel(pieces, *refs):
    joined_ref, near_sum_ref, far_sum_ref = refs[-3:]
    size = refs[0].shape[0]
    for spot, ref in enumerate(refs[:pieces]):
        joined_ref[spot * size : (spot + 1) * size, :] = ref[...]
    near_ref, far_ref, *shares = refs[pieces:-3]
    share = near_ref.shape[0]
    near_sum_ref[...] = tree([near_ref[...]] + [m[:share, :].astype(F32) for m in shares])
    far_sum_ref[...] = tree([far_ref[...]] + [m[share:, :].astype(F32) for m in shares]).astype(BF16)


def share_kernel(near_ref, far_ref, *refs):
    refs[-1][...] = (near_ref[...] + far_ref[...].astype(F32)).astype(BF16)


def table_kernel(place_ref, after_ref, *refs):
    del after_ref
    share = refs[0].shape[0]
    for step, ref in enumerate(refs[:-1]):
        spot = pl.multiple_of((place_ref[4] ^ step) * share, share)
        refs[-1][pl.ds(spot, share), :] = ref[...].astype(F32)


def body(table, owner, row, conv_weight, gain, upstream):
    shards, seqs = lax.axis_size("emb"), lax.axis_size("seq")
    seqs_dev, length = row.shape
    slab, width = table.shape
    layers, taps, _ = conv_weight.shape
    count = seqs_dev // MB * length
    capacity = max(2, 2 * count // shards)
    reach = MB * capacity
    wide = shards * capacity
    rows = layers * taps
    devices = shards * seqs
    axes = ("emb", "seq")

    low = log2(seqs)
    stages = [[low], [0, low + 1], [low + 2, low + 3]]
    left = [bit for bit in range(log2(devices)) if bit not in sum(stages, [])]
    me = lax.axis_index("emb") * seqs + lax.axis_index("seq")
    across = [log2(devices) - 1]
    group = list(range(low))
    peers = list(range(low, log2(devices) - 1))
    place = jnp.stack(
        [
            sum(((me >> bit) & 1) << spot for spot, bit in enumerate(bits))
            for bits in stages + [across, group, peers]
        ]
    ).astype(jnp.int32)

    def swap(value, bits, step):
        mask = sum(((step >> spot) & 1) << bit for spot, bit in enumerate(bits))
        return lax.ppermute(value, axes, [(i, i ^ mask) for i in range(devices)])

    near = shards // 2

    def exchange(value):
        groups = [list(range(near)), list(range(near, shards))]
        return lax.all_to_all(
            value, "emb", split_axis=0, concat_axis=0, axis_index_groups=groups, tiled=True
        )

    shape = jax.ShapeDtypeStruct
    held = functools.partial(pltpu.with_memory_space_constraint, memory_space=pltpu.HBM)
    mirrored = swap(table, across, 1)
    requests, codes, table = pl.pallas_call(
        functools.partial(request_kernel, slab),
        out_shape=(
            shape((near, 2 * reach), jnp.int32),
            shape((MB, count), jnp.int32),
            shape(table.shape, BF16),
        ),
        in_specs=[SMEM, VMEM, ANY],
        out_specs=(VMEM,) * 3,
        scratch_shapes=[pltpu.SemaphoreType.DMA],
        compiler_params=params(16),
        name="request",
    )(place, (owner[:, :, 0] * slab + row).reshape(MB, count), held(table))
    asked = exchange(requests)
    asked, *served = pl.pallas_call(
        near_kernel,
        out_shape=(shape(asked.shape, jnp.int32),) + (shape((reach, width), BF16),) * near,
        in_specs=[SMEM, VMEM, VMEM],
        out_specs=(VMEM,) * (1 + near),
        compiler_params=params(16),
        name="near",
    )(place, asked, table)
    served = pl.pallas_call(
        far_kernel,
        out_shape=(shape((2 * reach, width), BF16),) * near,
        in_specs=[VMEM] * (2 + near),
        out_specs=(VMEM,) * near,
        compiler_params=params(16),
        name="far",
    )(asked, mirrored, *served)
    order = ordered(near)
    fetched = [swap(served[step], peers, step) if step else served[0] for step in order]

    tokens = MB * count
    half = rows // 2
    padded = tokens + MB * PAD
    moved, keep, sent, block = pl.pallas_call(
        stack_kernel,
        out_shape=(
            shape((tokens, width), BF16),
            shape((half, width), BF16),
            shape((half + GROUP, width), BF16),
            shape((GROUP, width), BF16),
        ),
        in_specs=[SMEM, VMEM, VMEM, ANY, ANY] + [VMEM] * near,
        out_specs=(VMEM,) * 4,
        scratch_shapes=[
            pltpu.VMEM((tokens, width), F32),
            pltpu.VMEM((2, padded, width), F32),
            pltpu.VMEM((layers, tokens, width), BF16),
            pltpu.VMEM((layers, tokens, width), F32),
            pltpu.VMEM((layers, tokens, 128), F32),
            pltpu.VMEM((layers, tokens, width), F32),
            pltpu.VMEM((2, padded, width), F32),
            pltpu.VMEM((2, tokens, taps), BF16),
            pltpu.VMEM((rows, width), F32),
            pltpu.VMEM((layers, taps, width), BF16),
            pltpu.VMEM((layers, taps, width), BF16),
            pltpu.VMEM((layers, width), F32),
            pltpu.VMEM((tokens, width), BF16),
            pltpu.SemaphoreType.DMA((2,)),
        ],
        compiler_params=params(50),
        name="stack",
    )(
        place, codes.reshape(tokens, 1), conv_weight, held(gain),
        held(upstream.reshape(tokens, width)),
        *fetched,
    )

    chips = near // 2
    same, other = pl.pallas_call(
        place_kernel,
        out_shape=(shape((chips, 2 * reach, width), BF16),) * 2,
        in_specs=[VMEM, VMEM],
        out_specs=(VMEM, VMEM),
        compiler_params=params(24),
        name="place",
    )(codes, moved)
    other = swap(other, peers, 1)

    messages = [sent]
    share = slab // seqs
    for spot, bits in enumerate(stages[:-1]):
        arrived = [swap(message, bits, step + 1) for step, message in enumerate(messages)]
        parts = 2 ** len(stages[spot + 1])
        piece = keep.shape[0] // parts
        outs = (shape((piece, width), F32), shape((GROUP, width), BF16)) + (
            shape((piece + GROUP, width), BF16),
        ) * (parts - 1)
        rest = returned[1 : 1 + chips // 4] if spot == 1 else []
        keep, block, *messages = pl.pallas_call(
            functools.partial(fold_kernel, layers, len(arrived), parts, spot + 1),
            out_shape=outs,
            in_specs=[SMEM] + [VMEM] * (2 + len(arrived)) + [ANY] * len(rest),
            out_specs=(VMEM,) * len(outs),
            compiler_params=params(16),
            name=f"fold{spot}",
        )(place, keep, block, *arrived, *rest)
        if spot == 0:
            packed = pl.pallas_call(
                pack_kernel,
                out_shape=(shape((2, 2 * reach, width), BF16),) * chips,
                in_specs=[VMEM, VMEM, ANY],
                out_specs=(VMEM,) * chips,
                compiler_params=params(16),
                name="pack",
            )(same, other, block)
            returned = [
                swap(packed[step], peers[1:], step) if step else packed[0]
                for step in returning(chips)
            ]

    scale = float(seqs_dev * length * devices) ** (-0.5)
    arrived = [swap(message, stages[2], step + 1) for step, message in enumerate(messages)]
    keep, gain_grad = pl.pallas_call(
        functools.partial(last_kernel, layers, scale),
        out_shape=(shape(keep.shape, BF16), shape((layers, width), F32)),
        in_specs=[VMEM] * (2 + len(arrived)),
        out_specs=(VMEM,) * 2,
        compiler_params=params(16),
        name="last",
    )(keep, block, *arrived)
    near_share, far_share, *shares = pl.pallas_call(
        collect_kernel,
        out_shape=(shape((share, width), F32),) * 2
        + (shape((2 * share, width), BF16),) * (seqs - 1),
        in_specs=[SMEM, VMEM, ANY] + [VMEM] * chips,
        out_specs=(VMEM,) * (1 + seqs),
        scratch_shapes=[pltpu.VMEM((2, slab, width), F32)],
        compiler_params=params(24),
        name="collect",
    )(place, asked, keep, *returned)
    shares = [swap(value, group, step + 1) for step, value in enumerate(shares)]
    for bit in left:
        keep = (keep.astype(F32) + swap(keep, [bit], 1).astype(F32)).astype(BF16)
        gain_grad = gain_grad + swap(gain_grad, [bit], 1)

    line = [keep] + [swap(keep, stages[2], step) for step in range(1, 2 ** len(stages[2]))]
    keep, near_share, far_share = pl.pallas_call(
        functools.partial(line_kernel, len(line)),
        out_shape=(
            shape((half // 4, width), BF16),
            shape((share, width), F32),
            shape((share, width), BF16),
        ),
        in_specs=[VMEM] * (len(line) + 2 + len(shares)),
        out_specs=(VMEM,) * 3,
        compiler_params=params(16),
        name="line",
    )(*line, near_share, far_share, *shares)
    far_share = swap(far_share, across, 1)
    square = [keep] + [swap(keep, stages[1], step) for step in range(1, 4)]
    other = [swap(value, stages[0], 1) for value in square]
    part = pl.pallas_call(
        share_kernel,
        out_shape=shape((share, width), BF16),
        in_specs=[VMEM, VMEM, ANY],
        out_specs=VMEM,
        compiler_params=params(16),
        name="share",
    )(near_share, far_share, square[3])
    weight_grad = pl.pallas_call(
        functools.partial(finish_kernel, 2 ** len(stages[2]), scale, 0),
        out_shape=shape((rows, width), F32),
        in_specs=[SMEM] + [VMEM] * 4,
        out_specs=ANY,
        scratch_shapes=[pltpu.VMEM((4, half // 4, width), F32), pltpu.SemaphoreType.DMA((4,))],
        compiler_params=params(16),
        name="finish0",
    )(place, *square)
    weight_grad, mark = pl.pallas_call(
        functools.partial(finish_kernel, 2 ** len(stages[2]), scale, 1),
        out_shape=(shape((rows, width), F32), shape((8, 128), F32)),
        in_specs=[SMEM] + [VMEM] * 4 + [ANY],
        out_specs=(ANY, VMEM),
        scratch_shapes=[pltpu.VMEM((4, half // 4, width), F32), pltpu.SemaphoreType.DMA((4,))],
        input_output_aliases={5: 0},
        compiler_params=params(16),
        name="finish1",
    )(place, *other, weight_grad)
    table_grad = pl.pallas_call(
        table_kernel,
        out_shape=shape((slab, width), F32),
        in_specs=[SMEM, ANY] + [VMEM] * seqs,
        out_specs=VMEM,
        compiler_params=params(16),
        name="table",
    )(place, mark, part, *[swap(part, group, step) for step in range(1, seqs)])
    return (weight_grad.reshape(conv_weight.shape), gain_grad, table_grad)


def solution(mesh):
    in_specs = (
        P("emb", None),
        P(("emb", "seq"), None, None),
        P(("emb", "seq"), None),
        P(),
        P(),
        P(("emb", "seq"), None, None),
    )
    out_specs = (P(), P(), P("emb", None))
    return jax.shard_map(body, mesh=mesh, in_specs=in_specs, out_specs=out_specs, check_vma=False)
```

```python
import functools
import math

import jax
import jax.numpy as jnp
from jax import lax
from jax.experimental import pallas as pl
from jax.experimental.pallas import tpu as pltpu
from jax.sharding import PartitionSpec as P

MB = 2
TILE = 128
CHUNK = 128
PAD = 16
GROUP = 16
F32 = jnp.float32
BF16 = jnp.bfloat16
VMEM = pl.BlockSpec(memory_space=pltpu.VMEM)
SMEM = pl.BlockSpec(memory_space=pltpu.SMEM)
ANY = pl.BlockSpec(memory_space=pl.ANY)


def iota(shape, axis):
    return lax.broadcasted_iota(jnp.int32, shape, axis)


def one_hot(mask):
    return jnp.where(mask, 1.0, 0.0).astype(BF16)


def dot(a, b, contract=(1, 0)):
    return lax.dot_general(
        a, b, (((contract[0],), (contract[1],)), ((), ())), preferred_element_type=F32
    )


def log2(number):
    return int(number).bit_length() - 1


def ordered(near):
    return [0] + sorted(
        range(1, near),
        key=lambda step: (bin(step).count("1") != 1, not step & 2 or step < 4, step),
    )


def returning(chips):
    return [0] + sorted(range(1, chips), key=lambda step: (step & 1, step))


def params(mib):
    return pltpu.CompilerParams(vmem_limit_bytes=mib * 2**20)


def request_kernel(
    slab, place_ref, ids_ref, table_hbm, request_ref, code_ref, table_ref, sem
):
    copy = pltpu.make_async_copy(table_hbm, table_ref, sem)
    copy.start()
    near = request_ref.shape[0]
    reach = request_ref.shape[1] // 2
    batches, count = ids_ref.shape
    capacity = reach // batches
    upper = one_hot(iota((count, count), 0) <= iota((count, count), 1))
    for batch in range(batches):
        ids = ids_ref[batch : batch + 1, :]
        owners, rows = ids >> log2(slab), ids & (slab - 1)
        peers = owners & (near - 1)
        sides = (owners >> log2(near)) ^ place_ref[3]
        marks = jnp.where(iota((2 * near, count), 0) == sides * near + peers, 1.0, 0.0)
        ranks = dot(marks.astype(BF16), upper)
        slots = (jnp.sum(marks * ranks, axis=0, keepdims=True) - 1.0).astype(jnp.int32)
        code_ref[batch : batch + 1, :] = ((peers ^ place_ref[5]) * 2 + sides) * capacity + slots
        spots = one_hot(iota((capacity, count), 0) == slots)
        high = (marks * (rows >> 8).astype(F32)).astype(BF16)
        low = (marks * (rows & 255).astype(F32)).astype(BF16)
        asked = dot(high, spots, (1, 1)) * 256.0 + dot(low, spots, (1, 1))
        for side in range(2):
            start = side * reach + batch * capacity
            request_ref[:, start : start + capacity] = asked[
                side * near : (side + 1) * near
            ].astype(jnp.int32)
    copy.wait()


def near_kernel(place_ref, asked_ref, table_ref, turned_ref, *served_refs):
    near, both = asked_ref.shape
    reach = both // 2
    slab = table_ref.shape[0]
    asked = jnp.concatenate(
        [asked_ref[pl.ds(place_ref[5] ^ step, 1), :] for step in range(near)], axis=0
    )
    turned_ref[...] = asked
    columns = jnp.transpose(asked.astype(F32)).astype(jnp.int32)
    for step, served_ref in enumerate(served_refs):
        picks = one_hot(columns[:reach, step : step + 1] == iota((reach, slab), 1))
        served_ref[...] = dot(picks, table_ref[...]).astype(BF16)


def far_kernel(asked_ref, table_ref, *refs):
    near, both = asked_ref.shape
    reach = both // 2
    slab = table_ref.shape[0]
    columns = jnp.transpose(asked_ref[...].astype(F32)).astype(jnp.int32)
    for step in range(near):
        picks = one_hot(columns[reach:, step : step + 1] == iota((reach, slab), 1))
        refs[near + step][:reach, :] = refs[step][...]
        refs[near + step][reach:, :] = dot(picks, table_ref[...]).astype(BF16)


def collect_kernel(place_ref, asked_ref, after_ref, *refs):
    del after_ref
    near, both = asked_ref.shape
    reach = both // 2
    order = returning(near // 2)
    returned, refs = [refs[order.index(chip)] for chip in range(near // 2)], refs[near // 2 :]
    keeps, messages, parts_s = refs[:2], refs[2:-1], refs[-1]
    slab = parts_s.shape[1]
    share = slab // (1 + len(messages))
    for side in range(2):
        span = slice(side * reach, (side + 1) * reach)
        picks = [
            one_hot(iota((slab, reach), 0) == asked_ref[peer : peer + 1, span])
            for peer in range(near)
        ]
        rows = [ref[core, span, :] for ref in returned for core in range(2)]
        total = None
        pair = 2 if reach % 128 == 0 else 1
        for spot in range(0, near, pair):
            term = dot(
                jnp.concatenate(picks[spot : spot + pair], axis=1),
                jnp.concatenate(rows[spot : spot + pair], axis=0),
            )
            total = term if total is None else total + term
        parts_s[side] = total
        for step in range(1 + len(messages)):
            spot = pl.multiple_of((place_ref[4] ^ step) * share, share)
            value = parts_s[side, pl.ds(spot, share), :]
            if step == 0:
                keeps[side][...] = value
            else:
                messages[step - 1][side * share : (side + 1) * share, :] = value.astype(BF16)


def gain_block(values):
    high = values.astype(BF16)
    low = (values - high.astype(F32)).astype(BF16)
    rest = GROUP - 2 * values.shape[0]
    return jnp.concatenate([high, low, jnp.zeros((rest, values.shape[1]), BF16)], axis=0)


def gain_values(block, layers):
    blockf = block.astype(F32)
    return blockf[:layers] + blockf[layers : 2 * layers]


def stack_kernel(
    place_ref, column_ref, weight_hbm, gain_hbm, upstream_hbm, *refs,
):
    arrived_refs, refs = refs[:-19], refs[-19:]
    gain_ref, upstream_ref, weight_ref, sems = refs[15:]
    copies = [
        pltpu.make_async_copy(gain_hbm, gain_ref, sems.at[0]),
        pltpu.make_async_copy(upstream_hbm, upstream_ref, sems.at[1]),
    ] + [
        pltpu.make_async_copy(weight_hbm.at[layer], weight_ref.at[layer], sems.at[2 + layer])
        for layer in range(weight_ref.shape[0])
    ]
    for copy in copies:
        copy.start()
    order = ordered(len(arrived_refs))
    fetched_refs = [arrived_refs[order.index(step)] for step in range(len(order))]
    g_ref, keep_ref, sent_ref, block_ref = refs[:4]
    x_s, h_s, hidden_s, normed_s, inverse_s, slope_s, dconv_s, spread_s, dw_s = refs[4:13]
    rounded_s, turned_s = refs[13:15]
    layers, taps, width = weight_ref.shape
    shards, reach = 2 * len(fetched_refs), fetched_refs[0].shape[0] // 2
    tokens = column_ref.shape[0]
    batches = MB
    length = tokens // batches
    capacity = reach // batches
    wide = shards * capacity
    per = length // CHUNK
    steps = taps // width

    def at(seq, j):
        return pl.ds(seq * length + j * CHUNK, CHUNK)

    def inside(seq, j, ahead, size=CHUNK):
        return pl.ds(seq * (length + PAD) + j * CHUNK + ahead, size)

    for batch in range(batches):
        start = batch * (length + PAD)
        for side in range(2):
            h_s[side, start : start + PAD, :] = jnp.zeros((PAD, width), F32)
            dconv_s[side, start + length : start + length + PAD, :] = jnp.zeros((PAD, width), F32)
    dw_s[...] = jnp.zeros(dw_s.shape, F32)

    copies[0].wait()

    def normalise(seq, j, layer, value):
        centred = value - jnp.mean(value, axis=-1, keepdims=True)
        inverse = lax.rsqrt(jnp.mean(centred * centred, axis=-1, keepdims=True) + 1e-05)
        normed = centred * inverse
        normed_s[layer, at(seq, j), :] = normed
        inverse_s[layer, at(seq, j), :] = jnp.broadcast_to(inverse, (CHUNK, 128))
        hidden = normed * gain_ref[layer : layer + 1, :]
        h_s[layer % 2, inside(seq, j, PAD), :] = hidden
        hidden_s[layer, at(seq, j), :] = hidden.astype(BF16)

    for batch in range(batches):
        held = jnp.concatenate(
            [
                ref[side * reach + batch * capacity : side * reach + (batch + 1) * capacity, :]
                for ref in fetched_refs
                for side in range(2)
            ],
            axis=0,
        )
        for j in range(per):
            picks = one_hot(column_ref[at(batch, j), :] == iota((CHUNK, wide), 1))
            value = dot(picks, held)
            x_s[at(batch, j), :] = value
            normalise(batch, j, 0, value)

    root = math.sqrt(2.0 / math.pi)
    for layer in range(layers):
        dilation = 2**layer
        copies[2 + layer].wait()
        for start in range(0, taps, width):
            value = weight_ref[layer, start : start + width, :]
            rounded_s[layer, start : start + width, :] = value.astype(BF16)
            turned_s[layer, start : start + width, :] = jnp.transpose(value).astype(BF16)

        for seq in range(batches):
            for j in range(per):
                view = h_s[layer % 2, inside(seq, j, 0, CHUNK + PAD), :]
                stacked = jnp.concatenate(
                    [
                        view[PAD - tap * dilation : PAD - tap * dilation + CHUNK].astype(BF16)
                        for tap in range(steps)
                    ],
                    axis=1,
                )
                conv = dot(stacked, rounded_s[layer])
                square = conv * conv
                curve = jnp.tanh(conv * (root + (0.044715 * root) * square))
                half = 0.5 + 0.5 * curve
                gelu = conv * half
                slope_s[layer, at(seq, j), :] = half + gelu * (1.0 - curve) * (
                    root + (3.0 * 0.044715 * root) * square
                )
                if layer + 1 < layers:
                    value = (x_s[at(seq, j), :] + gelu).astype(BF16).astype(F32)
                    x_s[at(seq, j), :] = value
                    normalise(seq, j, layer + 1, value)

    def weigh(seq, layer):
        whole = pl.ds(seq * length, length)
        term = dot(hidden_s[layer, whole, :], spread_s[layer % 2, whole, :], (0, 0))
        for tap in range(steps):
            rows = pl.ds(layer * taps + tap * width, width)
            dw_s[rows, :] += term[:, tap * width : (tap + 1) * width]

    copies[1].wait()
    for seq in range(batches):
        for j in range(per):
            cotangent = upstream_ref[at(seq, j), :].astype(F32)
            dconv = (cotangent * slope_s[layers - 1, at(seq, j), :]).astype(BF16).astype(F32)
            dconv_s[(layers - 1) % 2, inside(seq, j, 0), :] = dconv

    gains = [None] * layers
    for layer in reversed(range(layers)):
        dilation = 2**layer

        total = jnp.zeros((8, width), F32)
        for seq in range(batches):
            if layer + 1 < layers:
                weigh(seq, layer + 1)
            for j in range(per):
                view = dconv_s[layer % 2, inside(seq, j, 0, CHUNK + PAD), :]
                spread = jnp.concatenate(
                    [
                        view[tap * dilation : tap * dilation + CHUNK].astype(BF16)
                        for tap in range(steps)
                    ],
                    axis=1,
                )
                spread_s[layer % 2, at(seq, j), :] = spread
                dhidden = dot(spread, turned_s[layer])
                normed = normed_s[layer, at(seq, j), :]
                product = dhidden * normed
                gain_row = gain_ref[layer : layer + 1, :]
                dnorm = dhidden * gain_row
                middle = jnp.mean(dnorm, axis=-1, keepdims=True)
                along = jnp.mean(product * gain_row, axis=-1, keepdims=True)
                inverse = inverse_s[layer, at(seq, j), :]
                inverse = jnp.concatenate([inverse] * (width // 128), axis=1)
                held = upstream_ref if layer == layers - 1 else g_ref
                cotangent = held[at(seq, j), :].astype(F32) + inverse * (
                    dnorm - middle - normed * along
                )
                cotangent = cotangent.astype(BF16)
                g_ref[at(seq, j), :] = cotangent
                if layer > 0:
                    dconv = cotangent.astype(F32) * slope_s[layer - 1, at(seq, j), :]
                    dconv_s[(layer - 1) % 2, inside(seq, j, 0), :] = dconv.astype(BF16).astype(F32)
                total = total + jnp.sum(product.reshape(CHUNK // 8, 8, width), axis=0)
        gains[layer] = jnp.sum(total, axis=0, keepdims=True)

    for batch in range(batches):
        weigh(batch, 0)
    half = keep_ref.shape[0]
    mine = place_ref[0]
    keep_ref[...] = dw_s[pl.ds(pl.multiple_of(mine * half, half), half), :].astype(BF16)
    sent_ref[:half, :] = dw_s[pl.ds(pl.multiple_of((1 - mine) * half, half), half), :].astype(BF16)
    block = gain_block(jnp.concatenate(gains, axis=0))
    sent_ref[half:, :] = block
    block_ref[...] = block


def place_kernel(code_ref, value_ref, *outgoing_refs):
    chips = outgoing_refs[0].shape[0]
    reach = outgoing_refs[0].shape[1] // 2
    batches, length = code_ref.shape
    capacity = reach // batches
    span = TILE // capacity
    for batch in range(batches):
        codes = code_ref[batch : batch + 1, :]
        whole = value_ref[batch * length : (batch + 1) * length, :]
        for j in range(4 * chips // span):
            picks = one_hot(iota((TILE, length), 0) + j * TILE == codes)
            rows = dot(picks, whole).astype(BF16)
            for spot in range(span):
                peer, side = divmod(j * span + spot, 2)
                start = side * reach + batch * capacity
                outgoing_refs[peer % 2][peer // 2, start : start + capacity, :] = rows[
                    spot * capacity : (spot + 1) * capacity
                ]


def pack_kernel(same_ref, other_ref, after_ref, *packed_refs):
    del after_ref
    for chip, ref in enumerate(packed_refs):
        ref[0] = same_ref[chip]
        ref[1] = other_ref[chip]


def tree(values):
    values = list(values)
    while len(values) > 1:
        values = [values[i] + values[i + 1] for i in range(0, len(values), 2)]
    return values[0]


def fold_kernel(layers, arrived, parts, spot, place_ref, keep_ref, block_ref, *refs):
    messages, outs = refs[:arrived], refs[-1 - parts :]
    size = keep_ref.shape[0]
    block = tree(
        [gain_values(block_ref[...], layers)]
        + [gain_values(message[size:, :], layers) for message in messages]
    )
    block = gain_block(block)
    piece = size // parts
    mine = place_ref[spot]
    for part in range(parts):
        rows = pl.ds(pl.multiple_of((mine ^ part) * piece, piece), piece)
        value = tree([keep_ref[rows, :].astype(F32)] + [m[rows, :].astype(F32) for m in messages])
        if part == 0:
            outs[0][...] = value
        else:
            outs[1 + part][:piece, :] = value.astype(BF16)
            outs[1 + part][piece:, :] = block
    outs[1][...] = block


def last_kernel(layers, scale, keep_ref, block_ref, *refs):
    messages, outs = refs[:-2], refs[-2:]
    size = keep_ref.shape[0]
    outs[0][...] = tree([keep_ref[...]] + [m[:size, :].astype(F32) for m in messages]).astype(BF16)
    block = tree(
        [gain_values(block_ref[...], layers)]
        + [gain_values(message[size:, :], layers) for message in messages]
    )
    outs[1][...] = block * scale


def finish_kernel(line, scale, side, place_ref, *refs):
    rows_s, sems = refs[-2:]
    out_ref = refs[-3 - side]
    square, block, _ = rows_s.shape
    piece = block // line
    copies = []
    for outer, ref in enumerate(refs[:square]):
        for inner in range(line):
            target = pl.multiple_of((place_ref[2] ^ inner) * piece, piece)
            rows_s[outer, pl.ds(target, piece), :] = (
                ref[inner * piece : (inner + 1) * piece, :].astype(F32) * scale
            )
        spot = (place_ref[0] ^ side) * square + (place_ref[1] ^ outer)
        rows = pl.ds(pl.multiple_of(spot * block, block), block)
        copies.append(pltpu.make_async_copy(rows_s.at[outer], out_ref.at[rows, :], sems.at[outer]))
        copies[-1].start()
    if side == 1:
        refs[-3][...] = jnp.zeros(refs[-3].shape, F32)
    for copy in copies:
        copy.wait()


def line_kernel(*refs):
    size = refs[0].shape[0]
    for spot, ref in enumerate(refs[:-1]):
        refs[-1][spot * size : (spot + 1) * size, :] = ref[...]


def shares_kernel(after_ref, near_ref, far_ref, *refs):
    del after_ref
    shares, (near_sum_ref, far_sum_ref) = refs[:-2], refs[-2:]
    share = near_ref.shape[0]
    near_sum_ref[...] = tree([near_ref[...]] + [m[:share, :].astype(F32) for m in shares])
    far_sum_ref[...] = tree([far_ref[...]] + [m[share:, :].astype(F32) for m in shares]).astype(BF16)


def share_kernel(near_ref, far_ref, *refs):
    refs[-1][...] = (near_ref[...] + far_ref[...].astype(F32)).astype(BF16)


def table_kernel(place_ref, after_ref, *refs):
    del after_ref
    share = refs[0].shape[0]
    for step, ref in enumerate(refs[:-1]):
        spot = pl.multiple_of((place_ref[4] ^ step) * share, share)
        refs[-1][pl.ds(spot, share), :] = ref[...].astype(F32)


def body(table, owner, row, conv_weight, gain, upstream):
    shards, seqs = lax.axis_size("emb"), lax.axis_size("seq")
    seqs_dev, length = row.shape
    slab, width = table.shape
    layers, taps, _ = conv_weight.shape
    count = seqs_dev // MB * length
    capacity = max(2, 2 * count // shards)
    reach = MB * capacity
    wide = shards * capacity
    rows = layers * taps
    devices = shards * seqs
    axes = ("emb", "seq")

    low = log2(seqs)
    stages = [[low], [0, low + 1], [low + 2, low + 3]]
    left = [bit for bit in range(log2(devices)) if bit not in sum(stages, [])]
    me = lax.axis_index("emb") * seqs + lax.axis_index("seq")
    across = [log2(devices) - 1]
    group = list(range(low))
    peers = list(range(low, log2(devices) - 1))
    place = jnp.stack(
        [
            sum(((me >> bit) & 1) << spot for spot, bit in enumerate(bits))
            for bits in stages + [across, group, peers]
        ]
    ).astype(jnp.int32)

    def swap(value, bits, step):
        mask = sum(((step >> spot) & 1) << bit for spot, bit in enumerate(bits))
        return lax.ppermute(value, axes, [(i, i ^ mask) for i in range(devices)])

    near = shards // 2

    def exchange(value):
        groups = [list(range(near)), list(range(near, shards))]
        return lax.all_to_all(
            value, "emb", split_axis=0, concat_axis=0, axis_index_groups=groups, tiled=True
        )

    shape = jax.ShapeDtypeStruct
    held = functools.partial(pltpu.with_memory_space_constraint, memory_space=pltpu.HBM)
    mirrored = swap(table, across, 1)
    requests, codes, table = pl.pallas_call(
        functools.partial(request_kernel, slab),
        out_shape=(
            shape((near, 2 * reach), jnp.int32),
            shape((MB, count), jnp.int32),
            shape(table.shape, BF16),
        ),
        in_specs=[SMEM, VMEM, ANY],
        out_specs=(VMEM,) * 3,
        scratch_shapes=[pltpu.SemaphoreType.DMA],
        compiler_params=params(16),
        name="request",
    )(place, (owner[:, :, 0] * slab + row).reshape(MB, count), held(table))
    asked = exchange(requests)
    asked, *served = pl.pallas_call(
        near_kernel,
        out_shape=(shape(asked.shape, jnp.int32),) + (shape((reach, width), BF16),) * near,
        in_specs=[SMEM, VMEM, VMEM],
        out_specs=(VMEM,) * (1 + near),
        compiler_params=params(16),
        name="near",
    )(place, asked, table)
    served = pl.pallas_call(
        far_kernel,
        out_shape=(shape((2 * reach, width), BF16),) * near,
        in_specs=[VMEM] * (2 + near),
        out_specs=(VMEM,) * near,
        compiler_params=params(16),
        name="far",
    )(asked, mirrored, *served)
    order = ordered(near)
    fetched = [swap(served[step], peers, step) if step else served[0] for step in order]

    tokens = MB * count
    half = rows // 2
    padded = tokens + MB * PAD
    moved, keep, sent, block = pl.pallas_call(
        stack_kernel,
        out_shape=(
            shape((tokens, width), BF16),
            shape((half, width), BF16),
            shape((half + GROUP, width), BF16),
            shape((GROUP, width), BF16),
        ),
        in_specs=[SMEM, VMEM, ANY, ANY, ANY] + [VMEM] * near,
        out_specs=(VMEM,) * 4,
        scratch_shapes=[
            pltpu.VMEM((tokens, width), F32),
            pltpu.VMEM((2, padded, width), F32),
            pltpu.VMEM((layers, tokens, width), BF16),
            pltpu.VMEM((layers, tokens, width), F32),
            pltpu.VMEM((layers, tokens, 128), F32),
            pltpu.VMEM((layers, tokens, width), F32),
            pltpu.VMEM((2, padded, width), F32),
            pltpu.VMEM((2, tokens, taps), BF16),
            pltpu.VMEM((rows, width), F32),
            pltpu.VMEM((layers, taps, width), BF16),
            pltpu.VMEM((layers, taps, width), BF16),
            pltpu.VMEM((layers, width), F32),
            pltpu.VMEM((tokens, width), BF16),
            pltpu.VMEM((layers, taps, width), F32),
            pltpu.SemaphoreType.DMA((2 + layers,)),
        ],
        compiler_params=params(40),
        name="stack",
    )(
        place, codes.reshape(tokens, 1), held(conv_weight), held(gain),
        held(upstream.reshape(tokens, width)),
        *fetched,
    )

    chips = near // 2
    same, other = pl.pallas_call(
        place_kernel,
        out_shape=(shape((chips, 2 * reach, width), BF16),) * 2,
        in_specs=[VMEM, VMEM],
        out_specs=(VMEM, VMEM),
        compiler_params=params(24),
        name="place",
    )(codes, moved)
    other = swap(other, peers, 1)

    messages = [sent]
    share = slab // seqs
    for spot, bits in enumerate(stages[:-1]):
        arrived = [swap(message, bits, step + 1) for step, message in enumerate(messages)]
        parts = 2 ** len(stages[spot + 1])
        piece = keep.shape[0] // parts
        outs = (shape((piece, width), F32), shape((GROUP, width), BF16)) + (
            shape((piece + GROUP, width), BF16),
        ) * (parts - 1)
        rest = returned[1 : 1 + chips // 4] if spot == 1 else []
        keep, block, *messages = pl.pallas_call(
            functools.partial(fold_kernel, layers, len(arrived), parts, spot + 1),
            out_shape=outs,
            in_specs=[SMEM] + [VMEM] * (2 + len(arrived)) + [ANY] * len(rest),
            out_specs=(VMEM,) * len(outs),
            compiler_params=params(16),
            name=f"fold{spot}",
        )(place, keep, block, *arrived, *rest)
        if spot == 0:
            packed = pl.pallas_call(
                pack_kernel,
                out_shape=(shape((2, 2 * reach, width), BF16),) * chips,
                in_specs=[VMEM, VMEM, ANY],
                out_specs=(VMEM,) * chips,
                compiler_params=params(16),
                name="pack",
            )(same, other, block)
            returned = [
                swap(packed[step], peers[1:], step) if step else packed[0]
                for step in returning(chips)
            ]

    scale = float(seqs_dev * length * devices) ** (-0.5)
    arrived = [swap(message, stages[2], step + 1) for step, message in enumerate(messages)]
    keep, gain_grad = pl.pallas_call(
        functools.partial(last_kernel, layers, scale),
        out_shape=(shape(keep.shape, BF16), shape((layers, width), F32)),
        in_specs=[VMEM] * (2 + len(arrived)),
        out_specs=(VMEM,) * 2,
        compiler_params=params(16),
        name="last",
    )(keep, block, *arrived)
    near_share, far_share, *shares = pl.pallas_call(
        collect_kernel,
        out_shape=(shape((share, width), F32),) * 2
        + (shape((2 * share, width), BF16),) * (seqs - 1),
        in_specs=[SMEM, VMEM, ANY] + [VMEM] * chips,
        out_specs=(VMEM,) * (1 + seqs),
        scratch_shapes=[pltpu.VMEM((2, slab, width), F32)],
        compiler_params=params(24),
        name="collect",
    )(place, asked, keep, *returned)
    shares = [swap(value, group, step + 1) for step, value in enumerate(shares)]
    for bit in left:
        keep = (keep.astype(F32) + swap(keep, [bit], 1).astype(F32)).astype(BF16)
        gain_grad = gain_grad + swap(gain_grad, [bit], 1)

    line = [keep] + [swap(keep, stages[2], step) for step in range(1, 2 ** len(stages[2]))]
    keep = pl.pallas_call(
        line_kernel,
        out_shape=shape((half // 4, width), BF16),
        in_specs=[VMEM] * len(line),
        out_specs=VMEM,
        compiler_params=params(16),
        name="line",
    )(*line)
    near_share, far_share = pl.pallas_call(
        shares_kernel,
        out_shape=(shape((share, width), F32), shape((share, width), BF16)),
        in_specs=[ANY] + [VMEM] * (2 + len(shares)),
        out_specs=(VMEM,) * 2,
        compiler_params=params(16),
        name="shares",
    )(keep, near_share, far_share, *shares)
    far_share = swap(far_share, across, 1)
    square = [keep] + [swap(keep, stages[1], step) for step in range(1, 4)]
    other = [swap(value, stages[0], 1) for value in square]
    part = pl.pallas_call(
        share_kernel,
        out_shape=shape((share, width), BF16),
        in_specs=[VMEM, VMEM, ANY],
        out_specs=VMEM,
        compiler_params=params(16),
        name="share",
    )(near_share, far_share, square[3])
    weight_grad = pl.pallas_call(
        functools.partial(finish_kernel, 2 ** len(stages[2]), scale, 0),
        out_shape=shape((rows, width), F32),
        in_specs=[SMEM] + [VMEM] * 4,
        out_specs=ANY,
        scratch_shapes=[pltpu.VMEM((4, half // 4, width), F32), pltpu.SemaphoreType.DMA((4,))],
        compiler_params=params(16),
        name="finish0",
    )(place, *square)
    weight_grad, mark = pl.pallas_call(
        functools.partial(finish_kernel, 2 ** len(stages[2]), scale, 1),
        out_shape=(shape((rows, width), F32), shape((8, 128), F32)),
        in_specs=[SMEM] + [VMEM] * 4 + [ANY],
        out_specs=(ANY, VMEM),
        scratch_shapes=[pltpu.VMEM((4, half // 4, width), F32), pltpu.SemaphoreType.DMA((4,))],
        input_output_aliases={5: 0},
        compiler_params=params(16),
        name="finish1",
    )(place, *other, weight_grad)
    table_grad = pl.pallas_call(
        table_kernel,
        out_shape=shape((slab, width), F32),
        in_specs=[SMEM, ANY] + [VMEM] * seqs,
        out_specs=VMEM,
        compiler_params=params(16),
        name="table",
    )(place, mark, part, *[swap(part, group, step) for step in range(1, seqs)])
    return (weight_grad.reshape(conv_weight.shape), gain_grad, table_grad)


def solution(mesh):
    in_specs = (
        P("emb", None),
        P(("emb", "seq"), None, None),
        P(("emb", "seq"), None),
        P(),
        P(),
        P(("emb", "seq"), None, None),
    )
    out_specs = (P(), P(), P("emb", None))
    return jax.shard_map(body, mesh=mesh, in_specs=in_specs, out_specs=out_specs, check_vma=False)
```

```python
import functools
import math

import jax
import jax.numpy as jnp
from jax import lax
from jax.experimental import pallas as pl
from jax.experimental.pallas import tpu as pltpu
from jax.sharding import PartitionSpec as P

MB = 2
TILE = 128
CHUNK = 128
PAD = 16
GROUP = 16
F32 = jnp.float32
BF16 = jnp.bfloat16
VMEM = pl.BlockSpec(memory_space=pltpu.VMEM)
SMEM = pl.BlockSpec(memory_space=pltpu.SMEM)
ANY = pl.BlockSpec(memory_space=pl.ANY)


def iota(shape, axis):
    return lax.broadcasted_iota(jnp.int32, shape, axis)


def one_hot(mask):
    return jnp.where(mask, 1.0, 0.0).astype(BF16)


def dot(a, b, contract=(1, 0)):
    return lax.dot_general(
        a, b, (((contract[0],), (contract[1],)), ((), ())), preferred_element_type=F32
    )


def log2(number):
    return int(number).bit_length() - 1


def ordered(near):
    top = near // 2
    steps = sorted(range(1, near), key=lambda step: (step < 2, step & 1, step < top, step < top + 2))
    return [0] + steps


def returning(chips):
    return [0] + sorted(range(1, chips), key=lambda step: (step & 1, step))


def params(mib):
    return pltpu.CompilerParams(vmem_limit_bytes=mib * 2**20)


def request_kernel(
    slab, place_ref, ids_ref, table_hbm, request_ref, code_ref, table_ref, sem
):
    copy = pltpu.make_async_copy(table_hbm, table_ref, sem)
    copy.start()
    near = request_ref.shape[0]
    reach = request_ref.shape[1] // 2
    batches, count = ids_ref.shape
    capacity = reach // batches
    upper = one_hot(iota((count, count), 0) <= iota((count, count), 1))
    for batch in range(batches):
        ids = ids_ref[batch : batch + 1, :]
        owners, rows = ids >> log2(slab), ids & (slab - 1)
        peers = owners & (near - 1)
        sides = (owners >> log2(near)) ^ place_ref[3]
        marks = jnp.where(iota((2 * near, count), 0) == sides * near + peers, 1.0, 0.0)
        ranks = dot(marks.astype(BF16), upper)
        slots = (jnp.sum(marks * ranks, axis=0, keepdims=True) - 1.0).astype(jnp.int32)
        code_ref[batch : batch + 1, :] = ((peers ^ place_ref[5]) * 2 + sides) * capacity + slots
        spots = one_hot(iota((capacity, count), 0) == slots)
        high = (marks * (rows >> 8).astype(F32)).astype(BF16)
        low = (marks * (rows & 255).astype(F32)).astype(BF16)
        asked = dot(high, spots, (1, 1)) * 256.0 + dot(low, spots, (1, 1))
        for side in range(2):
            start = side * reach + batch * capacity
            request_ref[:, start : start + capacity] = asked[
                side * near : (side + 1) * near
            ].astype(jnp.int32)
    copy.wait()


def near_kernel(place_ref, asked_ref, table_ref, turned_ref, *served_refs):
    near, both = asked_ref.shape
    reach = both // 2
    slab = table_ref.shape[0]
    asked = jnp.concatenate(
        [asked_ref[pl.ds(place_ref[5] ^ step, 1), :] for step in range(near)], axis=0
    )
    turned_ref[...] = asked
    columns = jnp.transpose(asked.astype(F32)).astype(jnp.int32)
    for step, served_ref in enumerate(served_refs):
        picks = one_hot(columns[:reach, step : step + 1] == iota((reach, slab), 1))
        served_ref[...] = dot(picks, table_ref[...]).astype(BF16)


def far_kernel(asked_ref, table_ref, *refs):
    near, both = asked_ref.shape
    reach = both // 2
    slab = table_ref.shape[0]
    columns = jnp.transpose(asked_ref[...].astype(F32)).astype(jnp.int32)
    for step in range(near):
        picks = one_hot(columns[reach:, step : step + 1] == iota((reach, slab), 1))
        refs[near + step][:reach, :] = refs[step][...]
        refs[near + step][reach:, :] = dot(picks, table_ref[...]).astype(BF16)


def collect_kernel(place_ref, asked_ref, after_ref, *refs):
    del after_ref
    near, both = asked_ref.shape
    reach = both // 2
    order = returning(near // 2)
    returned, refs = [refs[order.index(chip)] for chip in range(near // 2)], refs[near // 2 :]
    keeps, messages, parts_s = refs[:2], refs[2:-1], refs[-1]
    slab = parts_s.shape[1]
    share = slab // (1 + len(messages))
    for side in range(2):
        span = slice(side * reach, (side + 1) * reach)
        picks = [
            one_hot(iota((slab, reach), 0) == asked_ref[peer : peer + 1, span])
            for peer in range(near)
        ]
        rows = [ref[core, span, :] for ref in returned for core in range(2)]
        total = None
        pair = 2 if reach % 128 == 0 else 1
        for spot in range(0, near, pair):
            term = dot(
                jnp.concatenate(picks[spot : spot + pair], axis=1),
                jnp.concatenate(rows[spot : spot + pair], axis=0),
            )
            total = term if total is None else total + term
        parts_s[side] = total
        for step in range(1 + len(messages)):
            spot = pl.multiple_of((place_ref[4] ^ step) * share, share)
            value = parts_s[side, pl.ds(spot, share), :]
            if step == 0:
                keeps[side][...] = value
            else:
                messages[step - 1][side * share : (side + 1) * share, :] = value.astype(BF16)


def gain_block(values):
    high = values.astype(BF16)
    low = (values - high.astype(F32)).astype(BF16)
    rest = GROUP - 2 * values.shape[0]
    return jnp.concatenate([high, low, jnp.zeros((rest, values.shape[1]), BF16)], axis=0)


def gain_values(block, layers):
    blockf = block.astype(F32)
    return blockf[:layers] + blockf[layers : 2 * layers]


def stack_kernel(
    place_ref, column_ref, weight_hbm, gain_hbm, upstream_hbm, *refs,
):
    arrived_refs, refs = refs[:-19], refs[-19:]
    gain_ref, upstream_ref, weight_ref, sems = refs[15:]
    copies = [
        pltpu.make_async_copy(gain_hbm, gain_ref, sems.at[0]),
        *(
            pltpu.make_async_copy(weight_hbm.at[layer], weight_ref.at[layer], sems.at[2 + layer])
            for layer in range(weight_ref.shape[0])
        ),
        pltpu.make_async_copy(upstream_hbm, upstream_ref, sems.at[1]),
    ]
    for copy in copies:
        copy.start()
    order = ordered(len(arrived_refs))
    fetched_refs = [arrived_refs[order.index(step)] for step in range(len(order))]
    g_ref, keep_ref, sent_ref, block_ref = refs[:4]
    x_s, h_s, hidden_s, normed_s, inverse_s, slope_s, dconv_s, spread_s, dw_s = refs[4:13]
    rounded_s, turned_s = refs[13:15]
    layers, taps, width = weight_ref.shape
    shards, reach = 2 * len(fetched_refs), fetched_refs[0].shape[0] // 2
    tokens = column_ref.shape[0]
    batches = MB
    length = tokens // batches
    capacity = reach // batches
    wide = shards * capacity
    per = length // CHUNK
    steps = taps // width

    def at(seq, j):
        return pl.ds(seq * length + j * CHUNK, CHUNK)

    def inside(seq, j, ahead, size=CHUNK):
        return pl.ds(seq * (length + PAD) + j * CHUNK + ahead, size)

    for batch in range(batches):
        start = batch * (length + PAD)
        for side in range(2):
            h_s[side, start : start + PAD, :] = jnp.zeros((PAD, width), F32)
            dconv_s[side, start + length : start + length + PAD, :] = jnp.zeros((PAD, width), F32)
    dw_s[...] = jnp.zeros(dw_s.shape, F32)

    copies[0].wait()

    def normalise(seq, j, layer, value):
        centred = value - jnp.mean(value, axis=-1, keepdims=True)
        inverse = lax.rsqrt(jnp.mean(centred * centred, axis=-1, keepdims=True) + 1e-05)
        normed = centred * inverse
        normed_s[layer, at(seq, j), :] = normed
        inverse_s[layer, at(seq, j), :] = jnp.broadcast_to(inverse, (CHUNK, 128))
        hidden = normed * gain_ref[layer : layer + 1, :]
        h_s[layer % 2, inside(seq, j, PAD), :] = hidden
        hidden_s[layer, at(seq, j), :] = hidden.astype(BF16)

    for batch in range(batches):
        held = jnp.concatenate(
            [
                ref[side * reach + batch * capacity : side * reach + (batch + 1) * capacity, :]
                for ref in fetched_refs
                for side in range(2)
            ],
            axis=0,
        )
        for j in range(per):
            picks = one_hot(column_ref[at(batch, j), :] == iota((CHUNK, wide), 1))
            value = dot(picks, held)
            x_s[at(batch, j), :] = value
            normalise(batch, j, 0, value)

    root = math.sqrt(2.0 / math.pi)
    for layer in range(layers):
        dilation = 2**layer
        copies[1 + layer].wait()
        for start in range(0, taps, width):
            value = weight_ref[layer, start : start + width, :]
            rounded_s[layer, start : start + width, :] = value.astype(BF16)
            turned_s[layer, start : start + width, :] = jnp.transpose(value).astype(BF16)

        for seq in range(batches):
            for j in range(per):
                view = h_s[layer % 2, inside(seq, j, 0, CHUNK + PAD), :]
                stacked = jnp.concatenate(
                    [
                        view[PAD - tap * dilation : PAD - tap * dilation + CHUNK].astype(BF16)
                        for tap in range(steps)
                    ],
                    axis=1,
                )
                conv = dot(stacked, rounded_s[layer])
                square = conv * conv
                curve = jnp.tanh(conv * (root + (0.044715 * root) * square))
                half = 0.5 + 0.5 * curve
                gelu = conv * half
                slope_s[layer, at(seq, j), :] = half + gelu * (1.0 - curve) * (
                    root + (3.0 * 0.044715 * root) * square
                )
                if layer + 1 < layers:
                    value = (x_s[at(seq, j), :] + gelu).astype(BF16).astype(F32)
                    x_s[at(seq, j), :] = value
                    normalise(seq, j, layer + 1, value)

    def weigh(seq, layer):
        whole = pl.ds(seq * length, length)
        term = dot(hidden_s[layer, whole, :], spread_s[layer % 2, whole, :], (0, 0))
        for tap in range(steps):
            rows = pl.ds(layer * taps + tap * width, width)
            dw_s[rows, :] += term[:, tap * width : (tap + 1) * width]

    copies[-1].wait()
    for seq in range(batches):
        for j in range(per):
            cotangent = upstream_ref[at(seq, j), :].astype(F32)
            dconv = (cotangent * slope_s[layers - 1, at(seq, j), :]).astype(BF16).astype(F32)
            dconv_s[(layers - 1) % 2, inside(seq, j, 0), :] = dconv

    gains = [None] * layers
    for layer in reversed(range(layers)):
        dilation = 2**layer

        total = jnp.zeros((8, width), F32)
        for seq in range(batches):
            if layer + 1 < layers:
                weigh(seq, layer + 1)
            for j in range(per):
                view = dconv_s[layer % 2, inside(seq, j, 0, CHUNK + PAD), :]
                spread = jnp.concatenate(
                    [
                        view[tap * dilation : tap * dilation + CHUNK].astype(BF16)
                        for tap in range(steps)
                    ],
                    axis=1,
                )
                spread_s[layer % 2, at(seq, j), :] = spread
                dhidden = dot(spread, turned_s[layer])
                normed = normed_s[layer, at(seq, j), :]
                product = dhidden * normed
                gain_row = gain_ref[layer : layer + 1, :]
                dnorm = dhidden * gain_row
                middle = jnp.mean(dnorm, axis=-1, keepdims=True)
                along = jnp.mean(product * gain_row, axis=-1, keepdims=True)
                inverse = inverse_s[layer, at(seq, j), :]
                inverse = jnp.concatenate([inverse] * (width // 128), axis=1)
                held = upstream_ref if layer == layers - 1 else g_ref
                cotangent = held[at(seq, j), :].astype(F32) + inverse * (
                    dnorm - middle - normed * along
                )
                cotangent = cotangent.astype(BF16)
                g_ref[at(seq, j), :] = cotangent
                if layer > 0:
                    dconv = cotangent.astype(F32) * slope_s[layer - 1, at(seq, j), :]
                    dconv_s[(layer - 1) % 2, inside(seq, j, 0), :] = dconv.astype(BF16).astype(F32)
                total = total + jnp.sum(product.reshape(CHUNK // 8, 8, width), axis=0)
        gains[layer] = jnp.sum(total, axis=0, keepdims=True)

    for batch in range(batches):
        weigh(batch, 0)
    half = keep_ref.shape[0]
    mine = place_ref[0]
    keep_ref[...] = dw_s[pl.ds(pl.multiple_of(mine * half, half), half), :].astype(BF16)
    sent_ref[:half, :] = dw_s[pl.ds(pl.multiple_of((1 - mine) * half, half), half), :].astype(BF16)
    block = gain_block(jnp.concatenate(gains, axis=0))
    sent_ref[half:, :] = block
    block_ref[...] = block


def place_kernel(code_ref, value_ref, *outgoing_refs):
    chips = outgoing_refs[0].shape[0]
    reach = outgoing_refs[0].shape[1] // 2
    batches, length = code_ref.shape
    capacity = reach // batches
    span = TILE // capacity
    for batch in range(batches):
        codes = code_ref[batch : batch + 1, :]
        whole = value_ref[batch * length : (batch + 1) * length, :]
        for j in range(4 * chips // span):
            picks = one_hot(iota((TILE, length), 0) + j * TILE == codes)
            rows = dot(picks, whole).astype(BF16)
            for spot in range(span):
                peer, side = divmod(j * span + spot, 2)
                start = side * reach + batch * capacity
                outgoing_refs[peer % 2][peer // 2, start : start + capacity, :] = rows[
                    spot * capacity : (spot + 1) * capacity
                ]


def pack_kernel(same_ref, other_ref, after_ref, *packed_refs):
    del after_ref
    for chip, ref in enumerate(packed_refs):
        ref[0] = same_ref[chip]
        ref[1] = other_ref[chip]


def tree(values):
    values = list(values)
    while len(values) > 1:
        values = [values[i] + values[i + 1] for i in range(0, len(values), 2)]
    return values[0]


def fold_kernel(layers, arrived, parts, spot, place_ref, keep_ref, block_ref, *refs):
    messages, outs = refs[:arrived], refs[-1 - parts :]
    size = keep_ref.shape[0]
    block = tree(
        [gain_values(block_ref[...], layers)]
        + [gain_values(message[size:, :], layers) for message in messages]
    )
    block = gain_block(block)
    piece = size // parts
    mine = place_ref[spot]
    for part in range(parts):
        rows = pl.ds(pl.multiple_of((mine ^ part) * piece, piece), piece)
        value = tree([keep_ref[rows, :].astype(F32)] + [m[rows, :].astype(F32) for m in messages])
        if part == 0:
            outs[0][...] = value
        else:
            outs[1 + part][:piece, :] = value.astype(BF16)
            outs[1 + part][piece:, :] = block
    outs[1][...] = block


def last_kernel(layers, scale, keep_ref, block_ref, *refs):
    messages, outs = refs[:-2], refs[-2:]
    size = keep_ref.shape[0]
    outs[0][...] = tree([keep_ref[...]] + [m[:size, :].astype(F32) for m in messages]).astype(BF16)
    block = tree(
        [gain_values(block_ref[...], layers)]
        + [gain_values(message[size:, :], layers) for message in messages]
    )
    outs[1][...] = block * scale


def finish_kernel(line, scale, spots, place_ref, *refs):
    rows_s, sems = refs[-2:]
    first = len(refs) == len(spots) + 3
    out_ref = refs[-3 if first else -4]
    block = rows_s.shape[1]
    piece = block // line
    copies = []
    for number, (side, outer) in enumerate(spots):
        for inner in range(line):
            target = pl.multiple_of((place_ref[2] ^ inner) * piece, piece)
            rows_s[number, pl.ds(target, piece), :] = (
                refs[number][inner * piece : (inner + 1) * piece, :].astype(F32) * scale
            )
        spot = (place_ref[0] ^ side) * 4 + (place_ref[1] ^ outer)
        rows = pl.ds(pl.multiple_of(spot * block, block), block)
        copies.append(
            pltpu.make_async_copy(rows_s.at[number], out_ref.at[rows, :], sems.at[number])
        )
        copies[-1].start()
    if not first:
        refs[-3][...] = jnp.zeros(refs[-3].shape, F32)
    for copy in copies:
        copy.wait()


def line_kernel(*refs):
    size = refs[0].shape[0]
    for spot, ref in enumerate(refs[:-1]):
        refs[-1][spot * size : (spot + 1) * size, :] = ref[...]


def shares_kernel(after_ref, near_ref, far_ref, *refs):
    del after_ref
    shares, (near_sum_ref, far_sum_ref) = refs[:-2], refs[-2:]
    share = near_ref.shape[0]
    near_sum_ref[...] = tree([near_ref[...]] + [m[:share, :].astype(F32) for m in shares])
    far_sum_ref[...] = tree([far_ref[...]] + [m[share:, :].astype(F32) for m in shares]).astype(BF16)


def share_kernel(near_ref, far_ref, after_ref, part_ref):
    del after_ref
    part_ref[...] = (near_ref[...] + far_ref[...].astype(F32)).astype(BF16)


def table_kernel(place_ref, after_ref, *refs):
    del after_ref
    share = refs[0].shape[0]
    for step, ref in enumerate(refs[:-1]):
        spot = pl.multiple_of((place_ref[4] ^ step) * share, share)
        refs[-1][pl.ds(spot, share), :] = ref[...].astype(F32)


def body(table, owner, row, conv_weight, gain, upstream):
    shards, seqs = lax.axis_size("emb"), lax.axis_size("seq")
    seqs_dev, length = row.shape
    slab, width = table.shape
    layers, taps, _ = conv_weight.shape
    count = seqs_dev // MB * length
    capacity = max(2, 2 * count // shards)
    reach = MB * capacity
    wide = shards * capacity
    rows = layers * taps
    devices = shards * seqs
    axes = ("emb", "seq")

    low = log2(seqs)
    stages = [[low], [0, low + 1], [low + 2, low + 3]]
    left = [bit for bit in range(log2(devices)) if bit not in sum(stages, [])]
    me = lax.axis_index("emb") * seqs + lax.axis_index("seq")
    across = [log2(devices) - 1]
    group = list(range(low))
    peers = list(range(low, log2(devices) - 1))
    place = jnp.stack(
        [
            sum(((me >> bit) & 1) << spot for spot, bit in enumerate(bits))
            for bits in stages + [across, group, peers]
        ]
    ).astype(jnp.int32)

    def swap(value, bits, step):
        mask = sum(((step >> spot) & 1) << bit for spot, bit in enumerate(bits))
        return lax.ppermute(value, axes, [(i, i ^ mask) for i in range(devices)])

    near = shards // 2

    def exchange(value):
        groups = [list(range(near)), list(range(near, shards))]
        return lax.all_to_all(
            value, "emb", split_axis=0, concat_axis=0, axis_index_groups=groups, tiled=True
        )

    shape = jax.ShapeDtypeStruct
    held = functools.partial(pltpu.with_memory_space_constraint, memory_space=pltpu.HBM)
    mirrored = swap(table, across, 1)
    requests, codes, table = pl.pallas_call(
        functools.partial(request_kernel, slab),
        out_shape=(
            shape((near, 2 * reach), jnp.int32),
            shape((MB, count), jnp.int32),
            shape(table.shape, BF16),
        ),
        in_specs=[SMEM, VMEM, ANY],
        out_specs=(VMEM,) * 3,
        scratch_shapes=[pltpu.SemaphoreType.DMA],
        compiler_params=params(16),
        name="request",
    )(place, (owner[:, :, 0] * slab + row).reshape(MB, count), held(table))
    asked = exchange(requests)
    asked, *served = pl.pallas_call(
        near_kernel,
        out_shape=(shape(asked.shape, jnp.int32),) + (shape((reach, width), BF16),) * near,
        in_specs=[SMEM, VMEM, VMEM],
        out_specs=(VMEM,) * (1 + near),
        compiler_params=params(16),
        name="near",
    )(place, asked, table)
    served = pl.pallas_call(
        far_kernel,
        out_shape=(shape((2 * reach, width), BF16),) * near,
        in_specs=[VMEM] * (2 + near),
        out_specs=(VMEM,) * near,
        compiler_params=params(16),
        name="far",
    )(asked, mirrored, *served)
    order = ordered(near)
    fetched = [swap(served[step], peers, step) if step else served[0] for step in order]

    tokens = MB * count
    half = rows // 2
    padded = tokens + MB * PAD
    moved, keep, sent, block = pl.pallas_call(
        stack_kernel,
        out_shape=(
            shape((tokens, width), BF16),
            shape((half, width), BF16),
            shape((half + GROUP, width), BF16),
            shape((GROUP, width), BF16),
        ),
        in_specs=[SMEM, VMEM, ANY, ANY, ANY] + [VMEM] * near,
        out_specs=(VMEM,) * 4,
        scratch_shapes=[
            pltpu.VMEM((tokens, width), F32),
            pltpu.VMEM((2, padded, width), F32),
            pltpu.VMEM((layers, tokens, width), BF16),
            pltpu.VMEM((layers, tokens, width), F32),
            pltpu.VMEM((layers, tokens, 128), F32),
            pltpu.VMEM((layers, tokens, width), F32),
            pltpu.VMEM((2, padded, width), F32),
            pltpu.VMEM((2, tokens, taps), BF16),
            pltpu.VMEM((rows, width), F32),
            pltpu.VMEM((layers, taps, width), BF16),
            pltpu.VMEM((layers, taps, width), BF16),
            pltpu.VMEM((layers, width), F32),
            pltpu.VMEM((tokens, width), BF16),
            pltpu.VMEM((layers, taps, width), F32),
            pltpu.SemaphoreType.DMA((2 + layers,)),
        ],
        compiler_params=params(40),
        name="stack",
    )(
        place, codes.reshape(tokens, 1), held(conv_weight), held(gain),
        held(upstream.reshape(tokens, width)),
        *fetched,
    )

    chips = near // 2
    same, other = pl.pallas_call(
        place_kernel,
        out_shape=(shape((chips, 2 * reach, width), BF16),) * 2,
        in_specs=[VMEM, VMEM],
        out_specs=(VMEM, VMEM),
        compiler_params=params(24),
        name="place",
    )(codes, moved)
    other = swap(other, peers, 1)

    messages = [sent]
    share = slab // seqs
    for spot, bits in enumerate(stages[:-1]):
        arrived = [swap(message, bits, step + 1) for step, message in enumerate(messages)]
        parts = 2 ** len(stages[spot + 1])
        piece = keep.shape[0] // parts
        outs = (shape((piece, width), F32), shape((GROUP, width), BF16)) + (
            shape((piece + GROUP, width), BF16),
        ) * (parts - 1)
        rest = returned[1 : 1 + chips // 4] if spot == 1 else []
        keep, block, *messages = pl.pallas_call(
            functools.partial(fold_kernel, layers, len(arrived), parts, spot + 1),
            out_shape=outs,
            in_specs=[SMEM] + [VMEM] * (2 + len(arrived)) + [ANY] * len(rest),
            out_specs=(VMEM,) * len(outs),
            compiler_params=params(16),
            name=f"fold{spot}",
        )(place, keep, block, *arrived, *rest)
        if spot == 0:
            packed = pl.pallas_call(
                pack_kernel,
                out_shape=(shape((2, 2 * reach, width), BF16),) * chips,
                in_specs=[VMEM, VMEM, ANY],
                out_specs=(VMEM,) * chips,
                compiler_params=params(16),
                name="pack",
            )(same, other, block)
            returned = [
                swap(packed[step], peers[1:], step) if step else packed[0]
                for step in returning(chips)
            ]

    scale = float(seqs_dev * length * devices) ** (-0.5)
    arrived = [swap(message, stages[2], step + 1) for step, message in enumerate(messages)]
    keep, gain_grad = pl.pallas_call(
        functools.partial(last_kernel, layers, scale),
        out_shape=(shape(keep.shape, BF16), shape((layers, width), F32)),
        in_specs=[VMEM] * (2 + len(arrived)),
        out_specs=(VMEM,) * 2,
        compiler_params=params(16),
        name="last",
    )(keep, block, *arrived)
    near_share, far_share, *shares = pl.pallas_call(
        collect_kernel,
        out_shape=(shape((share, width), F32),) * 2
        + (shape((2 * share, width), BF16),) * (seqs - 1),
        in_specs=[SMEM, VMEM, ANY] + [VMEM] * chips,
        out_specs=(VMEM,) * (1 + seqs),
        scratch_shapes=[pltpu.VMEM((2, slab, width), F32)],
        compiler_params=params(24),
        name="collect",
    )(place, asked, keep, *returned)
    shares = [swap(value, group, step + 1) for step, value in enumerate(shares)]
    for bit in left:
        keep = (keep.astype(F32) + swap(keep, [bit], 1).astype(F32)).astype(BF16)
        gain_grad = gain_grad + swap(gain_grad, [bit], 1)

    line = [keep] + [swap(keep, stages[2], step) for step in range(1, 2 ** len(stages[2]))]
    keep = pl.pallas_call(
        line_kernel,
        out_shape=shape((half // 4, width), BF16),
        in_specs=[VMEM] * len(line),
        out_specs=VMEM,
        compiler_params=params(16),
        name="line",
    )(*line)
    near_share, far_share = pl.pallas_call(
        shares_kernel,
        out_shape=(shape((share, width), F32), shape((share, width), BF16)),
        in_specs=[ANY] + [VMEM] * (2 + len(shares)),
        out_specs=(VMEM,) * 2,
        compiler_params=params(16),
        name="shares",
    )(keep, near_share, far_share, *shares)
    far_share = swap(far_share, across, 1)
    square = [keep] + [swap(keep, stages[1], step) for step in range(1, 4)]
    other = [swap(value, stages[0], 1) for value in square]
    part = pl.pallas_call(
        share_kernel,
        out_shape=shape((share, width), BF16),
        in_specs=[VMEM, VMEM, ANY],
        out_specs=VMEM,
        compiler_params=params(16),
        name="share",
    )(near_share, far_share, square[3])
    pieces = [(side, outer) for side in range(2) for outer in range(4)]
    written = []
    for number, spots in enumerate((pieces[:5], pieces[5:])):
        written = pl.pallas_call(
            functools.partial(finish_kernel, 2 ** len(stages[2]), scale, spots),
            out_shape=(shape((rows, width), F32), shape((8, 128), F32))[: 1 + number],
            in_specs=[SMEM] + [VMEM] * len(spots) + [ANY] * number,
            out_specs=(ANY, VMEM)[: 1 + number],
            scratch_shapes=[
                pltpu.VMEM((len(spots), half // 4, width), F32),
                pltpu.SemaphoreType.DMA((len(spots),)),
            ],
            input_output_aliases={1 + len(spots): 0} if number else {},
            compiler_params=params(16),
            name=f"finish{number}",
        )(place, *[(square, other)[side][outer] for side, outer in spots], *written)
    weight_grad, mark = written
    table_grad = pl.pallas_call(
        table_kernel,
        out_shape=shape((slab, width), F32),
        in_specs=[SMEM, ANY] + [VMEM] * seqs,
        out_specs=VMEM,
        compiler_params=params(16),
        name="table",
    )(place, mark, part, *[swap(part, group, step) for step in range(1, seqs)])
    return (weight_grad.reshape(conv_weight.shape), gain_grad, table_grad)


def solution(mesh):
    in_specs = (
        P("emb", None),
        P(("emb", "seq"), None, None),
        P(("emb", "seq"), None),
        P(),
        P(),
        P(("emb", "seq"), None, None),
    )
    out_specs = (P(), P(), P("emb", None))
    return jax.shard_map(body, mesh=mesh, in_specs=in_specs, out_specs=out_specs, check_vma=False)
```

```python
import functools
import math

import jax
import jax.numpy as jnp
from jax import lax
from jax.experimental import pallas as pl
from jax.experimental.pallas import tpu as pltpu
from jax.sharding import PartitionSpec as P

MB = 2
TILE = 128
CHUNK = 128
PAD = 16
GROUP = 16
F32 = jnp.float32
BF16 = jnp.bfloat16
VMEM = pl.BlockSpec(memory_space=pltpu.VMEM)
SMEM = pl.BlockSpec(memory_space=pltpu.SMEM)
ANY = pl.BlockSpec(memory_space=pl.ANY)


def iota(shape, axis):
    return lax.broadcasted_iota(jnp.int32, shape, axis)


def one_hot(mask):
    return jnp.where(mask, 1.0, 0.0).astype(BF16)


def dot(a, b, contract=(1, 0)):
    return lax.dot_general(
        a, b, (((contract[0],), (contract[1],)), ((), ())), preferred_element_type=F32
    )


def log2(number):
    return int(number).bit_length() - 1


def ordered(near):
    top = near // 2
    steps = sorted(range(1, near), key=lambda step: (step < 2, step & 1, step < top, step < top + 2))
    return [0] + steps


def returning(chips):
    return [0] + sorted(range(1, chips), key=lambda step: (step & 1, step))


def params(mib):
    return pltpu.CompilerParams(vmem_limit_bytes=mib * 2**20)


def request_kernel(
    slab, place_ref, ids_ref, table_hbm, request_ref, code_ref, table_ref, sem
):
    copy = pltpu.make_async_copy(table_hbm, table_ref, sem)
    copy.start()
    near = request_ref.shape[0]
    reach = request_ref.shape[1] // 2
    batches, count = ids_ref.shape
    capacity = reach // batches
    upper = one_hot(iota((count, count), 0) <= iota((count, count), 1))
    for batch in range(batches):
        ids = ids_ref[batch : batch + 1, :]
        owners, rows = ids >> log2(slab), ids & (slab - 1)
        peers = owners & (near - 1)
        sides = (owners >> log2(near)) ^ place_ref[3]
        marks = jnp.where(iota((2 * near, count), 0) == sides * near + peers, 1.0, 0.0)
        ranks = dot(marks.astype(BF16), upper)
        slots = (jnp.sum(marks * ranks, axis=0, keepdims=True) - 1.0).astype(jnp.int32)
        code_ref[batch : batch + 1, :] = ((peers ^ place_ref[5]) * 2 + sides) * capacity + slots
        spots = one_hot(iota((capacity, count), 0) == slots)
        high = (marks * (rows >> 8).astype(F32)).astype(BF16)
        low = (marks * (rows & 255).astype(F32)).astype(BF16)
        asked = dot(high, spots, (1, 1)) * 256.0 + dot(low, spots, (1, 1))
        for side in range(2):
            start = side * reach + batch * capacity
            request_ref[:, start : start + capacity] = asked[
                side * near : (side + 1) * near
            ].astype(jnp.int32)
    copy.wait()


def near_kernel(place_ref, asked_ref, table_ref, turned_ref, *served_refs):
    near, both = asked_ref.shape
    reach = both // 2
    slab = table_ref.shape[0]
    asked = jnp.concatenate(
        [asked_ref[pl.ds(place_ref[5] ^ step, 1), :] for step in range(near)], axis=0
    )
    turned_ref[...] = asked
    columns = jnp.transpose(asked.astype(F32)).astype(jnp.int32)
    for step, served_ref in enumerate(served_refs):
        picks = one_hot(columns[:reach, step : step + 1] == iota((reach, slab), 1))
        served_ref[...] = dot(picks, table_ref[...]).astype(BF16)


def far_kernel(asked_ref, table_ref, *refs):
    near, both = asked_ref.shape
    reach = both // 2
    slab = table_ref.shape[0]
    columns = jnp.transpose(asked_ref[...].astype(F32)).astype(jnp.int32)
    for step in range(near):
        picks = one_hot(columns[reach:, step : step + 1] == iota((reach, slab), 1))
        refs[near + step][:reach, :] = refs[step][...]
        refs[near + step][reach:, :] = dot(picks, table_ref[...]).astype(BF16)


def collect_kernel(place_ref, asked_ref, after_ref, *refs):
    del after_ref
    near, both = asked_ref.shape
    reach = both // 2
    order = returning(near // 2)
    returned, refs = [refs[order.index(chip)] for chip in range(near // 2)], refs[near // 2 :]
    keeps, messages, parts_s = refs[:2], refs[2:-1], refs[-1]
    slab = parts_s.shape[1]
    share = slab // (1 + len(messages))
    for side in range(2):
        span = slice(side * reach, (side + 1) * reach)
        picks = [
            one_hot(iota((slab, reach), 0) == asked_ref[peer : peer + 1, span])
            for peer in range(near)
        ]
        rows = [ref[core, span, :] for ref in returned for core in range(2)]
        total = None
        pair = 2 if reach % 128 == 0 else 1
        for spot in range(0, near, pair):
            term = dot(
                jnp.concatenate(picks[spot : spot + pair], axis=1),
                jnp.concatenate(rows[spot : spot + pair], axis=0),
            )
            total = term if total is None else total + term
        parts_s[side] = total
        for step in range(1 + len(messages)):
            spot = pl.multiple_of((place_ref[4] ^ step) * share, share)
            value = parts_s[side, pl.ds(spot, share), :]
            if step == 0:
                keeps[side][...] = value
            else:
                messages[step - 1][side * share : (side + 1) * share, :] = value.astype(BF16)


def gain_block(values):
    high = values.astype(BF16)
    low = (values - high.astype(F32)).astype(BF16)
    rest = GROUP - 2 * values.shape[0]
    return jnp.concatenate([high, low, jnp.zeros((rest, values.shape[1]), BF16)], axis=0)


def gain_values(block, layers):
    blockf = block.astype(F32)
    return blockf[:layers] + blockf[layers : 2 * layers]


def stack_kernel(
    place_ref, column_ref, weight_hbm, gain_hbm, upstream_hbm, *refs,
):
    arrived_refs, refs = refs[:-19], refs[-19:]
    gain_ref, upstream_ref, weight_ref, sems = refs[15:]
    copies = [
        pltpu.make_async_copy(gain_hbm, gain_ref, sems.at[0]),
        *(
            pltpu.make_async_copy(weight_hbm.at[layer], weight_ref.at[layer], sems.at[2 + layer])
            for layer in range(weight_ref.shape[0])
        ),
        pltpu.make_async_copy(upstream_hbm, upstream_ref, sems.at[1]),
    ]
    copies[0].start()
    copies[1].start()
    order = ordered(len(arrived_refs))
    fetched_refs = [arrived_refs[order.index(step)] for step in range(len(order))]
    g_ref, keep_ref, sent_ref, block_ref = refs[:4]
    x_s, h_s, hidden_s, normed_s, inverse_s, slope_s, dconv_s, spread_s, dw_s = refs[4:13]
    rounded_s, turned_s = refs[13:15]
    layers, taps, width = weight_ref.shape
    shards, reach = 2 * len(fetched_refs), fetched_refs[0].shape[0] // 2
    tokens = column_ref.shape[0]
    batches = MB
    length = tokens // batches
    capacity = reach // batches
    wide = shards * capacity
    per = length // CHUNK
    steps = taps // width

    def at(seq, j):
        return pl.ds(seq * length + j * CHUNK, CHUNK)

    def inside(seq, j, ahead, size=CHUNK):
        return pl.ds(seq * (length + PAD) + j * CHUNK + ahead, size)

    for batch in range(batches):
        start = batch * (length + PAD)
        for side in range(2):
            h_s[side, start : start + PAD, :] = jnp.zeros((PAD, width), F32)
            dconv_s[side, start + length : start + length + PAD, :] = jnp.zeros((PAD, width), F32)

    copies[0].wait()

    def normalise(seq, j, layer, value):
        centred = value - jnp.mean(value, axis=-1, keepdims=True)
        inverse = lax.rsqrt(jnp.mean(centred * centred, axis=-1, keepdims=True) + 1e-05)
        normed = centred * inverse
        normed_s[layer, at(seq, j), :] = normed
        inverse_s[layer, at(seq, j), :] = jnp.broadcast_to(inverse, (CHUNK, 128))
        hidden = normed * gain_ref[layer : layer + 1, :]
        h_s[layer % 2, inside(seq, j, PAD), :] = hidden
        hidden_s[layer, at(seq, j), :] = hidden.astype(BF16)

    for batch in range(batches):
        held = jnp.concatenate(
            [
                ref[side * reach + batch * capacity : side * reach + (batch + 1) * capacity, :]
                for ref in fetched_refs
                for side in range(2)
            ],
            axis=0,
        )
        for j in range(per):
            picks = one_hot(column_ref[at(batch, j), :] == iota((CHUNK, wide), 1))
            value = dot(picks, held)
            x_s[at(batch, j), :] = value
            normalise(batch, j, 0, value)

    root = math.sqrt(2.0 / math.pi)
    for layer in range(layers):
        dilation = 2**layer
        copies[1 + layer].wait()
        if layer == 0:
            for copy in copies[2:]:
                copy.start()
        for start in range(0, taps, width):
            value = weight_ref[layer, start : start + width, :]
            rounded_s[layer, start : start + width, :] = value.astype(BF16)
            turned_s[layer, start : start + width, :] = jnp.transpose(value).astype(BF16)

        for seq in range(batches):
            for j in range(per):
                view = h_s[layer % 2, inside(seq, j, 0, CHUNK + PAD), :]
                stacked = jnp.concatenate(
                    [
                        view[PAD - tap * dilation : PAD - tap * dilation + CHUNK].astype(BF16)
                        for tap in range(steps)
                    ],
                    axis=1,
                )
                conv = dot(stacked, rounded_s[layer])
                square = conv * conv
                curve = jnp.tanh(conv * (root + (0.044715 * root) * square))
                half = 0.5 + 0.5 * curve
                gelu = conv * half
                slope_s[layer, at(seq, j), :] = half + gelu * (1.0 - curve) * (
                    root + (3.0 * 0.044715 * root) * square
                )
                if layer + 1 < layers:
                    value = (x_s[at(seq, j), :] + gelu).astype(BF16).astype(F32)
                    x_s[at(seq, j), :] = value
                    normalise(seq, j, layer + 1, value)

    def weigh(layer):
        term = dot(hidden_s[layer], spread_s[layer % 2], (0, 0))
        for tap in range(steps):
            rows = pl.ds(layer * taps + tap * width, width)
            dw_s[rows, :] = term[:, tap * width : (tap + 1) * width]

    copies[-1].wait()
    for seq in range(batches):
        for j in range(per):
            cotangent = upstream_ref[at(seq, j), :].astype(F32)
            dconv = (cotangent * slope_s[layers - 1, at(seq, j), :]).astype(BF16).astype(F32)
            dconv_s[(layers - 1) % 2, inside(seq, j, 0), :] = dconv

    gains = [None] * layers
    for layer in reversed(range(layers)):
        dilation = 2**layer

        total = jnp.zeros((8, width), F32)
        if layer + 1 < layers:
            weigh(layer + 1)
        for seq in range(batches):
            for j in range(per):
                view = dconv_s[layer % 2, inside(seq, j, 0, CHUNK + PAD), :]
                spread = jnp.concatenate(
                    [
                        view[tap * dilation : tap * dilation + CHUNK].astype(BF16)
                        for tap in range(steps)
                    ],
                    axis=1,
                )
                spread_s[layer % 2, at(seq, j), :] = spread
                dhidden = dot(spread, turned_s[layer])
                normed = normed_s[layer, at(seq, j), :]
                product = dhidden * normed
                gain_row = gain_ref[layer : layer + 1, :]
                dnorm = dhidden * gain_row
                middle = jnp.mean(dnorm, axis=-1, keepdims=True)
                along = jnp.mean(product * gain_row, axis=-1, keepdims=True)
                inverse = inverse_s[layer, at(seq, j), :]
                inverse = jnp.concatenate([inverse] * (width // 128), axis=1)
                held = upstream_ref if layer == layers - 1 else g_ref
                cotangent = held[at(seq, j), :].astype(F32) + inverse * (
                    dnorm - middle - normed * along
                )
                cotangent = cotangent.astype(BF16)
                g_ref[at(seq, j), :] = cotangent
                if layer > 0:
                    dconv = cotangent.astype(F32) * slope_s[layer - 1, at(seq, j), :]
                    dconv_s[(layer - 1) % 2, inside(seq, j, 0), :] = dconv.astype(BF16).astype(F32)
                total = total + jnp.sum(product.reshape(CHUNK // 8, 8, width), axis=0)
        gains[layer] = jnp.sum(total, axis=0, keepdims=True)

    weigh(0)
    half = keep_ref.shape[0]
    mine = place_ref[0]
    keep_ref[...] = dw_s[pl.ds(pl.multiple_of(mine * half, half), half), :].astype(BF16)
    sent_ref[:half, :] = dw_s[pl.ds(pl.multiple_of((1 - mine) * half, half), half), :].astype(BF16)
    block = gain_block(jnp.concatenate(gains, axis=0))
    sent_ref[half:, :] = block
    block_ref[...] = block


def place_kernel(code_ref, value_ref, *outgoing_refs):
    chips = outgoing_refs[0].shape[0]
    reach = outgoing_refs[0].shape[1] // 2
    batches, length = code_ref.shape
    capacity = reach // batches
    span = TILE // capacity
    for batch in range(batches):
        codes = code_ref[batch : batch + 1, :]
        whole = value_ref[batch * length : (batch + 1) * length, :]
        for j in range(4 * chips // span):
            picks = one_hot(iota((TILE, length), 0) + j * TILE == codes)
            rows = dot(picks, whole).astype(BF16)
            for spot in range(span):
                peer, side = divmod(j * span + spot, 2)
                start = side * reach + batch * capacity
                outgoing_refs[peer % 2][peer // 2, start : start + capacity, :] = rows[
                    spot * capacity : (spot + 1) * capacity
                ]


def pack_kernel(same_ref, other_ref, after_ref, *packed_refs):
    del after_ref
    for chip, ref in enumerate(packed_refs):
        ref[0] = same_ref[chip]
        ref[1] = other_ref[chip]


def tree(values):
    values = list(values)
    while len(values) > 1:
        values = [values[i] + values[i + 1] for i in range(0, len(values), 2)]
    return values[0]


def fold_kernel(layers, arrived, parts, spot, place_ref, keep_ref, block_ref, *refs):
    messages, outs = refs[:arrived], refs[-1 - parts :]
    size = keep_ref.shape[0]
    block = tree(
        [gain_values(block_ref[...], layers)]
        + [gain_values(message[size:, :], layers) for message in messages]
    )
    block = gain_block(block)
    piece = size // parts
    mine = place_ref[spot]
    for part in range(parts):
        rows = pl.ds(pl.multiple_of((mine ^ part) * piece, piece), piece)
        value = tree([keep_ref[rows, :].astype(F32)] + [m[rows, :].astype(F32) for m in messages])
        if part == 0:
            outs[0][...] = value
        else:
            outs[1 + part][:piece, :] = value.astype(BF16)
            outs[1 + part][piece:, :] = block
    outs[1][...] = block


def last_kernel(layers, scale, keep_ref, block_ref, *refs):
    messages, outs = refs[:-2], refs[-2:]
    size = keep_ref.shape[0]
    outs[0][...] = tree([keep_ref[...]] + [m[:size, :].astype(F32) for m in messages]).astype(BF16)
    block = tree(
        [gain_values(block_ref[...], layers)]
        + [gain_values(message[size:, :], layers) for message in messages]
    )
    outs[1][...] = block * scale


def finish_kernel(line, scale, spots, place_ref, *refs):
    rows_s, sems = refs[-2:]
    first = len(refs) == len(spots) + 3
    out_ref = refs[-3 if first else -4]
    block = rows_s.shape[1]
    piece = block // line
    copies = []
    for number, (side, outer) in enumerate(spots):
        for inner in range(line):
            target = pl.multiple_of((place_ref[2] ^ inner) * piece, piece)
            rows_s[number, pl.ds(target, piece), :] = (
                refs[number][inner * piece : (inner + 1) * piece, :].astype(F32) * scale
            )
        spot = (place_ref[0] ^ side) * 4 + (place_ref[1] ^ outer)
        rows = pl.ds(pl.multiple_of(spot * block, block), block)
        copies.append(
            pltpu.make_async_copy(rows_s.at[number], out_ref.at[rows, :], sems.at[number])
        )
        copies[-1].start()
    if not first:
        refs[-3][...] = jnp.zeros(refs[-3].shape, F32)
    for copy in copies:
        copy.wait()


def line_kernel(*refs):
    size = refs[0].shape[0]
    for spot, ref in enumerate(refs[:-1]):
        refs[-1][spot * size : (spot + 1) * size, :] = ref[...]


def shares_kernel(after_ref, near_ref, far_ref, *refs):
    del after_ref
    shares, (near_sum_ref, far_sum_ref) = refs[:-2], refs[-2:]
    share = near_ref.shape[0]
    near_sum_ref[...] = tree([near_ref[...]] + [m[:share, :].astype(F32) for m in shares])
    far_sum_ref[...] = tree([far_ref[...]] + [m[share:, :].astype(F32) for m in shares]).astype(BF16)


def share_kernel(near_ref, far_ref, after_ref, part_ref):
    del after_ref
    part_ref[...] = (near_ref[...] + far_ref[...].astype(F32)).astype(BF16)


def table_kernel(place_ref, after_ref, *refs):
    del after_ref
    share = refs[0].shape[0]
    for step, ref in enumerate(refs[:-1]):
        spot = pl.multiple_of((place_ref[4] ^ step) * share, share)
        refs[-1][pl.ds(spot, share), :] = ref[...].astype(F32)


def body(table, owner, row, conv_weight, gain, upstream):
    shards, seqs = lax.axis_size("emb"), lax.axis_size("seq")
    seqs_dev, length = row.shape
    slab, width = table.shape
    layers, taps, _ = conv_weight.shape
    count = seqs_dev // MB * length
    capacity = max(2, 2 * count // shards)
    reach = MB * capacity
    wide = shards * capacity
    rows = layers * taps
    devices = shards * seqs
    axes = ("emb", "seq")

    low = log2(seqs)
    stages = [[low], [0, low + 1], [low + 2, low + 3]]
    left = [bit for bit in range(log2(devices)) if bit not in sum(stages, [])]
    me = lax.axis_index("emb") * seqs + lax.axis_index("seq")
    across = [log2(devices) - 1]
    group = list(range(low))
    peers = list(range(low, log2(devices) - 1))
    place = jnp.stack(
        [
            sum(((me >> bit) & 1) << spot for spot, bit in enumerate(bits))
            for bits in stages + [across, group, peers]
        ]
    ).astype(jnp.int32)

    def swap(value, bits, step):
        mask = sum(((step >> spot) & 1) << bit for spot, bit in enumerate(bits))
        return lax.ppermute(value, axes, [(i, i ^ mask) for i in range(devices)])

    near = shards // 2

    def exchange(value):
        groups = [list(range(near)), list(range(near, shards))]
        return lax.all_to_all(
            value, "emb", split_axis=0, concat_axis=0, axis_index_groups=groups, tiled=True
        )

    shape = jax.ShapeDtypeStruct
    held = functools.partial(pltpu.with_memory_space_constraint, memory_space=pltpu.HBM)
    mirrored = swap(table, across, 1)
    requests, codes, table = pl.pallas_call(
        functools.partial(request_kernel, slab),
        out_shape=(
            shape((near, 2 * reach), jnp.int32),
            shape((MB, count), jnp.int32),
            shape(table.shape, BF16),
        ),
        in_specs=[SMEM, VMEM, ANY],
        out_specs=(VMEM,) * 3,
        scratch_shapes=[pltpu.SemaphoreType.DMA],
        compiler_params=params(16),
        name="request",
    )(place, (owner[:, :, 0] * slab + row).reshape(MB, count), held(table))
    asked = exchange(requests)
    asked, *served = pl.pallas_call(
        near_kernel,
        out_shape=(shape(asked.shape, jnp.int32),) + (shape((reach, width), BF16),) * near,
        in_specs=[SMEM, VMEM, VMEM],
        out_specs=(VMEM,) * (1 + near),
        compiler_params=params(16),
        name="near",
    )(place, asked, table)
    served = pl.pallas_call(
        far_kernel,
        out_shape=(shape((2 * reach, width), BF16),) * near,
        in_specs=[VMEM] * (2 + near),
        out_specs=(VMEM,) * near,
        compiler_params=params(16),
        name="far",
    )(asked, mirrored, *served)
    order = ordered(near)
    fetched = [swap(served[step], peers, step) if step else served[0] for step in order]

    tokens = MB * count
    half = rows // 2
    padded = tokens + MB * PAD
    moved, keep, sent, block = pl.pallas_call(
        stack_kernel,
        out_shape=(
            shape((tokens, width), BF16),
            shape((half, width), BF16),
            shape((half + GROUP, width), BF16),
            shape((GROUP, width), BF16),
        ),
        in_specs=[SMEM, VMEM, ANY, ANY, ANY] + [VMEM] * near,
        out_specs=(VMEM,) * 4,
        scratch_shapes=[
            pltpu.VMEM((tokens, width), F32),
            pltpu.VMEM((2, padded, width), F32),
            pltpu.VMEM((layers, tokens, width), BF16),
            pltpu.VMEM((layers, tokens, width), F32),
            pltpu.VMEM((layers, tokens, 128), F32),
            pltpu.VMEM((layers, tokens, width), F32),
            pltpu.VMEM((2, padded, width), F32),
            pltpu.VMEM((2, tokens, taps), BF16),
            pltpu.VMEM((rows, width), F32),
            pltpu.VMEM((layers, taps, width), BF16),
            pltpu.VMEM((layers, taps, width), BF16),
            pltpu.VMEM((layers, width), F32),
            pltpu.VMEM((tokens, width), BF16),
            pltpu.VMEM((layers, taps, width), F32),
            pltpu.SemaphoreType.DMA((2 + layers,)),
        ],
        compiler_params=params(40),
        name="stack",
    )(
        place, codes.reshape(tokens, 1), held(conv_weight), held(gain),
        held(upstream.reshape(tokens, width)),
        *fetched,
    )

    chips = near // 2
    same, other = pl.pallas_call(
        place_kernel,
        out_shape=(shape((chips, 2 * reach, width), BF16),) * 2,
        in_specs=[VMEM, VMEM],
        out_specs=(VMEM, VMEM),
        compiler_params=params(24),
        name="place",
    )(codes, moved)
    other = swap(other, peers, 1)

    messages = [sent]
    share = slab // seqs
    for spot, bits in enumerate(stages[:-1]):
        arrived = [swap(message, bits, step + 1) for step, message in enumerate(messages)]
        parts = 2 ** len(stages[spot + 1])
        piece = keep.shape[0] // parts
        outs = (shape((piece, width), F32), shape((GROUP, width), BF16)) + (
            shape((piece + GROUP, width), BF16),
        ) * (parts - 1)
        rest = returned[1 : 1 + chips // 4] if spot == 1 else []
        keep, block, *messages = pl.pallas_call(
            functools.partial(fold_kernel, layers, len(arrived), parts, spot + 1),
            out_shape=outs,
            in_specs=[SMEM] + [VMEM] * (2 + len(arrived)) + [ANY] * len(rest),
            out_specs=(VMEM,) * len(outs),
            compiler_params=params(16),
            name=f"fold{spot}",
        )(place, keep, block, *arrived, *rest)
        if spot == 0:
            packed = pl.pallas_call(
                pack_kernel,
                out_shape=(shape((2, 2 * reach, width), BF16),) * chips,
                in_specs=[VMEM, VMEM, ANY],
                out_specs=(VMEM,) * chips,
                compiler_params=params(16),
                name="pack",
            )(same, other, block)
            returned = [
                swap(packed[step], peers[1:], step) if step else packed[0]
                for step in returning(chips)
            ]

    scale = float(seqs_dev * length * devices) ** (-0.5)
    arrived = [swap(message, stages[2], step + 1) for step, message in enumerate(messages)]
    keep, gain_grad = pl.pallas_call(
        functools.partial(last_kernel, layers, scale),
        out_shape=(shape(keep.shape, BF16), shape((layers, width), F32)),
        in_specs=[VMEM] * (2 + len(arrived)),
        out_specs=(VMEM,) * 2,
        compiler_params=params(16),
        name="last",
    )(keep, block, *arrived)
    near_share, far_share, *shares = pl.pallas_call(
        collect_kernel,
        out_shape=(shape((share, width), F32),) * 2
        + (shape((2 * share, width), BF16),) * (seqs - 1),
        in_specs=[SMEM, VMEM, ANY] + [VMEM] * chips,
        out_specs=(VMEM,) * (1 + seqs),
        scratch_shapes=[pltpu.VMEM((2, slab, width), F32)],
        compiler_params=params(24),
        name="collect",
    )(place, asked, keep, *returned)
    shares = [swap(value, group, step + 1) for step, value in enumerate(shares)]
    for bit in left:
        keep = (keep.astype(F32) + swap(keep, [bit], 1).astype(F32)).astype(BF16)
        gain_grad = gain_grad + swap(gain_grad, [bit], 1)

    line = [keep] + [swap(keep, stages[2], step) for step in range(1, 2 ** len(stages[2]))]
    keep = pl.pallas_call(
        line_kernel,
        out_shape=shape((half // 4, width), BF16),
        in_specs=[VMEM] * len(line),
        out_specs=VMEM,
        compiler_params=params(16),
        name="line",
    )(*line)
    near_share, far_share = pl.pallas_call(
        shares_kernel,
        out_shape=(shape((share, width), F32), shape((share, width), BF16)),
        in_specs=[ANY] + [VMEM] * (2 + len(shares)),
        out_specs=(VMEM,) * 2,
        compiler_params=params(16),
        name="shares",
    )(keep, near_share, far_share, *shares)
    far_share = swap(far_share, across, 1)
    square = [keep] + [swap(keep, stages[1], step) for step in range(1, 4)]
    other = [swap(value, stages[0], 1) for value in square]
    part = pl.pallas_call(
        share_kernel,
        out_shape=shape((share, width), BF16),
        in_specs=[VMEM, VMEM, ANY],
        out_specs=VMEM,
        compiler_params=params(16),
        name="share",
    )(near_share, far_share, square[3])
    pieces = [(side, outer) for side in range(2) for outer in range(4)]
    written = []
    for number, spots in enumerate((pieces[:5], pieces[5:])):
        written = pl.pallas_call(
            functools.partial(finish_kernel, 2 ** len(stages[2]), scale, spots),
            out_shape=(shape((rows, width), F32), shape((8, 128), F32))[: 1 + number],
            in_specs=[SMEM] + [VMEM] * len(spots) + [ANY] * number,
            out_specs=(ANY, VMEM)[: 1 + number],
            scratch_shapes=[
                pltpu.VMEM((len(spots), half // 4, width), F32),
                pltpu.SemaphoreType.DMA((len(spots),)),
            ],
            input_output_aliases={1 + len(spots): 0} if number else {},
            compiler_params=params(16),
            name=f"finish{number}",
        )(place, *[(square, other)[side][outer] for side, outer in spots], *written)
    weight_grad, mark = written
    table_grad = pl.pallas_call(
        table_kernel,
        out_shape=shape((slab, width), F32),
        in_specs=[SMEM, ANY] + [VMEM] * seqs,
        out_specs=VMEM,
        compiler_params=params(16),
        name="table",
    )(place, mark, part, *[swap(part, group, step) for step in range(1, seqs)])
    return (weight_grad.reshape(conv_weight.shape), gain_grad, table_grad)


def solution(mesh):
    in_specs = (
        P("emb", None),
        P(("emb", "seq"), None, None),
        P(("emb", "seq"), None),
        P(),
        P(),
        P(("emb", "seq"), None, None),
    )
    out_specs = (P(), P(), P("emb", None))
    return jax.shard_map(body, mesh=mesh, in_specs=in_specs, out_specs=out_specs, check_vma=False)
```

```python
import functools
import math

import jax
import jax.numpy as jnp
from jax import lax
from jax.experimental import pallas as pl
from jax.experimental.pallas import tpu as pltpu
from jax.sharding import PartitionSpec as P

MB = 2
TILE = 128
CHUNK = 128
PAD = 16
GROUP = 16
F32 = jnp.float32
BF16 = jnp.bfloat16
VMEM = pl.BlockSpec(memory_space=pltpu.VMEM)
SMEM = pl.BlockSpec(memory_space=pltpu.SMEM)
ANY = pl.BlockSpec(memory_space=pl.ANY)


def iota(shape, axis):
    return lax.broadcasted_iota(jnp.int32, shape, axis)


def one_hot(mask):
    return jnp.where(mask, 1.0, 0.0).astype(BF16)


def dot(a, b, contract=(1, 0)):
    return lax.dot_general(
        a, b, (((contract[0],), (contract[1],)), ((), ())), preferred_element_type=F32
    )


def log2(number):
    return int(number).bit_length() - 1


def ordered(near):
    top = near // 2
    steps = sorted(range(1, near), key=lambda step: (step < 2, step & 1, step < top, step < top + 2))
    return [0] + steps


def returning(chips):
    return [0] + sorted(range(1, chips), key=lambda step: (step & 1, step))


def params(mib):
    return pltpu.CompilerParams(vmem_limit_bytes=mib * 2**20)


def request_kernel(
    slab, place_ref, ids_ref, table_hbm, request_ref, code_ref, table_ref, sem
):
    copy = pltpu.make_async_copy(table_hbm, table_ref, sem)
    copy.start()
    near = request_ref.shape[0]
    reach = request_ref.shape[1] // 2
    batches, count = ids_ref.shape
    capacity = reach // batches
    upper = one_hot(iota((count, count), 0) <= iota((count, count), 1))
    for batch in range(batches):
        ids = ids_ref[batch : batch + 1, :]
        owners, rows = ids >> log2(slab), ids & (slab - 1)
        peers = owners & (near - 1)
        sides = (owners >> log2(near)) ^ place_ref[3]
        marks = jnp.where(iota((2 * near, count), 0) == sides * near + peers, 1.0, 0.0)
        ranks = dot(marks.astype(BF16), upper)
        slots = (jnp.sum(marks * ranks, axis=0, keepdims=True) - 1.0).astype(jnp.int32)
        code_ref[batch : batch + 1, :] = ((peers ^ place_ref[5]) * 2 + sides) * capacity + slots
        spots = one_hot(iota((capacity, count), 0) == slots)
        high = (marks * (rows >> 8).astype(F32)).astype(BF16)
        low = (marks * (rows & 255).astype(F32)).astype(BF16)
        asked = dot(high, spots, (1, 1)) * 256.0 + dot(low, spots, (1, 1))
        for side in range(2):
            start = side * reach + batch * capacity
            request_ref[:, start : start + capacity] = asked[
                side * near : (side + 1) * near
            ].astype(jnp.int32)
    copy.wait()


def near_kernel(place_ref, asked_ref, table_ref, turned_ref, *served_refs):
    near, both = asked_ref.shape
    reach = both // 2
    slab = table_ref.shape[0]
    asked = jnp.concatenate(
        [asked_ref[pl.ds(place_ref[5] ^ step, 1), :] for step in range(near)], axis=0
    )
    turned_ref[...] = asked
    columns = jnp.transpose(asked.astype(F32)).astype(jnp.int32)
    for step, served_ref in enumerate(served_refs):
        picks = one_hot(columns[:reach, step : step + 1] == iota((reach, slab), 1))
        served_ref[...] = dot(picks, table_ref[...]).astype(BF16)


def far_kernel(asked_ref, table_ref, *refs):
    near, both = asked_ref.shape
    reach = both // 2
    slab = table_ref.shape[0]
    columns = jnp.transpose(asked_ref[...].astype(F32)).astype(jnp.int32)
    for step in range(near):
        picks = one_hot(columns[reach:, step : step + 1] == iota((reach, slab), 1))
        refs[near + step][:reach, :] = refs[step][...]
        refs[near + step][reach:, :] = dot(picks, table_ref[...]).astype(BF16)


def collect_kernel(place_ref, asked_ref, after_ref, *refs):
    del after_ref
    near, both = asked_ref.shape
    reach = both // 2
    order = returning(near // 2)
    returned, refs = [refs[order.index(chip)] for chip in range(near // 2)], refs[near // 2 :]
    keeps, messages, parts_s = refs[:2], refs[2:-1], refs[-1]
    slab = parts_s.shape[1]
    share = slab // (1 + len(messages))
    for side in range(2):
        span = slice(side * reach, (side + 1) * reach)
        picks = [
            one_hot(iota((slab, reach), 0) == asked_ref[peer : peer + 1, span])
            for peer in range(near)
        ]
        rows = [ref[core, span, :] for ref in returned for core in range(2)]
        total = None
        pair = 2 if reach % 128 == 0 else 1
        for spot in range(0, near, pair):
            term = dot(
                jnp.concatenate(picks[spot : spot + pair], axis=1),
                jnp.concatenate(rows[spot : spot + pair], axis=0),
            )
            total = term if total is None else total + term
        parts_s[side] = total
        for step in range(1 + len(messages)):
            spot = pl.multiple_of((place_ref[4] ^ step) * share, share)
            value = parts_s[side, pl.ds(spot, share), :]
            if step == 0:
                keeps[side][...] = value
            else:
                messages[step - 1][side * share : (side + 1) * share, :] = value.astype(BF16)


def weight_kernel(weight_hbm, rounded_ref, turned_ref, weight_s, sems):
    layers, taps, width = weight_s.shape
    copies = [
        pltpu.make_async_copy(weight_hbm.at[layer], weight_s.at[layer], sems.at[layer])
        for layer in range(layers)
    ]
    for copy in copies:
        copy.start()
    for layer in range(layers):
        copies[layer].wait()
        for start in range(0, taps, width):
            value = weight_s[layer, start : start + width, :]
            rounded_ref[layer, start : start + width, :] = value.astype(BF16)
            turned_ref[layer, start : start + width, :] = jnp.transpose(value).astype(BF16)


def gain_block(values):
    high = values.astype(BF16)
    low = (values - high.astype(F32)).astype(BF16)
    rest = GROUP - 2 * values.shape[0]
    return jnp.concatenate([high, low, jnp.zeros((rest, values.shape[1]), BF16)], axis=0)


def gain_values(block, layers):
    blockf = block.astype(F32)
    return blockf[:layers] + blockf[layers : 2 * layers]


def stack_kernel(
    place_ref, column_ref, rounded_ref, turned_ref, gain_hbm, upstream_hbm, *refs,
):
    arrived_refs, refs = refs[:-16], refs[-16:]
    gain_ref, upstream_ref, sems = refs[13:]
    copies = [
        pltpu.make_async_copy(gain_hbm, gain_ref, sems.at[0]),
        pltpu.make_async_copy(upstream_hbm, upstream_ref, sems.at[1]),
    ]
    for copy in copies:
        copy.start()
    order = ordered(len(arrived_refs))
    fetched_refs = [arrived_refs[order.index(step)] for step in range(len(order))]
    g_ref, keep_ref, sent_ref, block_ref = refs[:4]
    x_s, h_s, hidden_s, normed_s, inverse_s, slope_s, dconv_s, spread_s, dw_s = refs[4:13]
    layers, taps, width = rounded_ref.shape
    shards, reach = 2 * len(fetched_refs), fetched_refs[0].shape[0] // 2
    tokens = column_ref.shape[0]
    batches = MB
    length = tokens // batches
    capacity = reach // batches
    wide = shards * capacity
    per = length // CHUNK
    steps = taps // width

    def at(seq, j):
        return pl.ds(seq * length + j * CHUNK, CHUNK)

    def inside(seq, j, ahead, size=CHUNK):
        return pl.ds(seq * (length + PAD) + j * CHUNK + ahead, size)

    for batch in range(batches):
        start = batch * (length + PAD)
        for side in range(2):
            h_s[side, start : start + PAD, :] = jnp.zeros((PAD, width), F32)
            dconv_s[side, start + length : start + length + PAD, :] = jnp.zeros((PAD, width), F32)
    dw_s[...] = jnp.zeros(dw_s.shape, F32)

    copies[0].wait()

    def normalise(seq, j, layer, value):
        centred = value - jnp.mean(value, axis=-1, keepdims=True)
        inverse = lax.rsqrt(jnp.mean(centred * centred, axis=-1, keepdims=True) + 1e-05)
        normed = centred * inverse
        normed_s[layer, at(seq, j), :] = normed
        inverse_s[layer, at(seq, j), :] = jnp.broadcast_to(inverse, (CHUNK, 128))
        hidden = normed * gain_ref[layer : layer + 1, :]
        h_s[layer % 2, inside(seq, j, PAD), :] = hidden
        hidden_s[layer, at(seq, j), :] = hidden.astype(BF16)

    for batch in range(batches):
        held = jnp.concatenate(
            [
                ref[side * reach + batch * capacity : side * reach + (batch + 1) * capacity, :]
                for ref in fetched_refs
                for side in range(2)
            ],
            axis=0,
        )
        for j in range(per):
            picks = one_hot(column_ref[at(batch, j), :] == iota((CHUNK, wide), 1))
            value = dot(picks, held)
            x_s[at(batch, j), :] = value
            normalise(batch, j, 0, value)

    root = math.sqrt(2.0 / math.pi)
    for layer in range(layers):
        dilation = 2**layer

        for seq in range(batches):
            for j in range(per):
                view = h_s[layer % 2, inside(seq, j, 0, CHUNK + PAD), :]
                stacked = jnp.concatenate(
                    [
                        view[PAD - tap * dilation : PAD - tap * dilation + CHUNK].astype(BF16)
                        for tap in range(steps)
                    ],
                    axis=1,
                )
                conv = dot(stacked, rounded_ref[layer])
                square = conv * conv
                curve = jnp.tanh(conv * (root + (0.044715 * root) * square))
                half = 0.5 + 0.5 * curve
                gelu = conv * half
                slope_s[layer, at(seq, j), :] = half + gelu * (1.0 - curve) * (
                    root + (3.0 * 0.044715 * root) * square
                )
                if layer + 1 < layers:
                    value = (x_s[at(seq, j), :] + gelu).astype(BF16).astype(F32)
                    x_s[at(seq, j), :] = value
                    normalise(seq, j, layer + 1, value)

    def weigh(seq, layer):
        whole = pl.ds(seq * length, length)
        term = dot(hidden_s[layer, whole, :], spread_s[layer % 2, whole, :], (0, 0))
        for tap in range(steps):
            rows = pl.ds(layer * taps + tap * width, width)
            dw_s[rows, :] += term[:, tap * width : (tap + 1) * width]

    copies[-1].wait()
    for seq in range(batches):
        for j in range(per):
            cotangent = upstream_ref[at(seq, j), :].astype(F32)
            dconv = (cotangent * slope_s[layers - 1, at(seq, j), :]).astype(BF16).astype(F32)
            dconv_s[(layers - 1) % 2, inside(seq, j, 0), :] = dconv

    gains = [None] * layers
    for layer in reversed(range(layers)):
        dilation = 2**layer

        total = jnp.zeros((8, width), F32)
        for seq in range(batches):
            if layer + 1 < layers:
                weigh(seq, layer + 1)
            for j in range(per):
                view = dconv_s[layer % 2, inside(seq, j, 0, CHUNK + PAD), :]
                spread = jnp.concatenate(
                    [
                        view[tap * dilation : tap * dilation + CHUNK].astype(BF16)
                        for tap in range(steps)
                    ],
                    axis=1,
                )
                spread_s[layer % 2, at(seq, j), :] = spread
                dhidden = dot(spread, turned_ref[layer])
                normed = normed_s[layer, at(seq, j), :]
                product = dhidden * normed
                gain_row = gain_ref[layer : layer + 1, :]
                dnorm = dhidden * gain_row
                middle = jnp.mean(dnorm, axis=-1, keepdims=True)
                along = jnp.mean(product * gain_row, axis=-1, keepdims=True)
                inverse = inverse_s[layer, at(seq, j), :]
                inverse = jnp.concatenate([inverse] * (width // 128), axis=1)
                held = upstream_ref if layer == layers - 1 else g_ref
                cotangent = held[at(seq, j), :].astype(F32) + inverse * (
                    dnorm - middle - normed * along
                )
                cotangent = cotangent.astype(BF16)
                g_ref[at(seq, j), :] = cotangent
                if layer > 0:
                    dconv = cotangent.astype(F32) * slope_s[layer - 1, at(seq, j), :]
                    dconv_s[(layer - 1) % 2, inside(seq, j, 0), :] = dconv.astype(BF16).astype(F32)
                total = total + jnp.sum(product.reshape(CHUNK // 8, 8, width), axis=0)
        gains[layer] = jnp.sum(total, axis=0, keepdims=True)

    for batch in range(batches):
        weigh(batch, 0)
    half = keep_ref.shape[0]
    mine = place_ref[0]
    keep_ref[...] = dw_s[pl.ds(pl.multiple_of(mine * half, half), half), :].astype(BF16)
    sent_ref[:half, :] = dw_s[pl.ds(pl.multiple_of((1 - mine) * half, half), half), :].astype(BF16)
    block = gain_block(jnp.concatenate(gains, axis=0))
    sent_ref[half:, :] = block
    block_ref[...] = block


def place_kernel(code_ref, value_ref, *outgoing_refs):
    chips = outgoing_refs[0].shape[0]
    reach = outgoing_refs[0].shape[1] // 2
    batches, length = code_ref.shape
    capacity = reach // batches
    span = TILE // capacity
    for batch in range(batches):
        codes = code_ref[batch : batch + 1, :]
        whole = value_ref[batch * length : (batch + 1) * length, :]
        for j in range(4 * chips // span):
            picks = one_hot(iota((TILE, length), 0) + j * TILE == codes)
            rows = dot(picks, whole).astype(BF16)
            for spot in range(span):
                peer, side = divmod(j * span + spot, 2)
                start = side * reach + batch * capacity
                outgoing_refs[peer % 2][peer // 2, start : start + capacity, :] = rows[
                    spot * capacity : (spot + 1) * capacity
                ]


def pack_kernel(same_ref, other_ref, after_ref, *packed_refs):
    del after_ref
    for chip, ref in enumerate(packed_refs):
        ref[0] = same_ref[chip]
        ref[1] = other_ref[chip]


def tree(values):
    values = list(values)
    while len(values) > 1:
        values = [values[i] + values[i + 1] for i in range(0, len(values), 2)]
    return values[0]


def fold_kernel(layers, arrived, parts, spot, place_ref, keep_ref, block_ref, *refs):
    messages, outs = refs[:arrived], refs[-1 - parts :]
    size = keep_ref.shape[0]
    block = tree(
        [gain_values(block_ref[...], layers)]
        + [gain_values(message[size:, :], layers) for message in messages]
    )
    block = gain_block(block)
    piece = size // parts
    mine = place_ref[spot]
    for part in range(parts):
        rows = pl.ds(pl.multiple_of((mine ^ part) * piece, piece), piece)
        value = tree([keep_ref[rows, :].astype(F32)] + [m[rows, :].astype(F32) for m in messages])
        if part == 0:
            outs[0][...] = value
        else:
            outs[1 + part][:piece, :] = value.astype(BF16)
            outs[1 + part][piece:, :] = block
    outs[1][...] = block


def last_kernel(layers, scale, keep_ref, block_ref, *refs):
    messages, outs = refs[:-2], refs[-2:]
    size = keep_ref.shape[0]
    outs[0][...] = tree([keep_ref[...]] + [m[:size, :].astype(F32) for m in messages]).astype(BF16)
    block = tree(
        [gain_values(block_ref[...], layers)]
        + [gain_values(message[size:, :], layers) for message in messages]
    )
    outs[1][...] = block * scale


def finish_kernel(line, scale, spots, place_ref, *refs):
    rows_s, sems = refs[-2:]
    first = len(refs) == len(spots) + 3
    out_ref = refs[-3 if first else -4]
    block = rows_s.shape[1]
    piece = block // line
    copies = []
    for number, (side, outer) in enumerate(spots):
        for inner in range(line):
            target = pl.multiple_of((place_ref[2] ^ inner) * piece, piece)
            rows_s[number, pl.ds(target, piece), :] = (
                refs[number][inner * piece : (inner + 1) * piece, :].astype(F32) * scale
            )
        spot = (place_ref[0] ^ side) * 4 + (place_ref[1] ^ outer)
        rows = pl.ds(pl.multiple_of(spot * block, block), block)
        copies.append(
            pltpu.make_async_copy(rows_s.at[number], out_ref.at[rows, :], sems.at[number])
        )
        copies[-1].start()
    if not first:
        refs[-3][...] = jnp.zeros(refs[-3].shape, F32)
    for copy in copies:
        copy.wait()


def line_kernel(*refs):
    size = refs[0].shape[0]
    for spot, ref in enumerate(refs[:-1]):
        refs[-1][spot * size : (spot + 1) * size, :] = ref[...]


def shares_kernel(after_ref, near_ref, far_ref, *refs):
    del after_ref
    shares, (near_sum_ref, far_sum_ref) = refs[:-2], refs[-2:]
    share = near_ref.shape[0]
    near_sum_ref[...] = tree([near_ref[...]] + [m[:share, :].astype(F32) for m in shares])
    far_sum_ref[...] = tree([far_ref[...]] + [m[share:, :].astype(F32) for m in shares]).astype(BF16)


def share_kernel(near_ref, far_ref, after_ref, part_ref):
    del after_ref
    part_ref[...] = (near_ref[...] + far_ref[...].astype(F32)).astype(BF16)


def table_kernel(place_ref, after_ref, *refs):
    del after_ref
    share = refs[0].shape[0]
    for step, ref in enumerate(refs[:-1]):
        spot = pl.multiple_of((place_ref[4] ^ step) * share, share)
        refs[-1][pl.ds(spot, share), :] = ref[...].astype(F32)


def body(table, owner, row, conv_weight, gain, upstream):
    shards, seqs = lax.axis_size("emb"), lax.axis_size("seq")
    seqs_dev, length = row.shape
    slab, width = table.shape
    layers, taps, _ = conv_weight.shape
    count = seqs_dev // MB * length
    capacity = max(2, 2 * count // shards)
    reach = MB * capacity
    wide = shards * capacity
    rows = layers * taps
    devices = shards * seqs
    axes = ("emb", "seq")

    low = log2(seqs)
    stages = [[low], [0, low + 1], [low + 2, low + 3]]
    left = [bit for bit in range(log2(devices)) if bit not in sum(stages, [])]
    me = lax.axis_index("emb") * seqs + lax.axis_index("seq")
    across = [log2(devices) - 1]
    group = list(range(low))
    peers = list(range(low, log2(devices) - 1))
    place = jnp.stack(
        [
            sum(((me >> bit) & 1) << spot for spot, bit in enumerate(bits))
            for bits in stages + [across, group, peers]
        ]
    ).astype(jnp.int32)

    def swap(value, bits, step):
        mask = sum(((step >> spot) & 1) << bit for spot, bit in enumerate(bits))
        return lax.ppermute(value, axes, [(i, i ^ mask) for i in range(devices)])

    near = shards // 2

    def exchange(value):
        groups = [list(range(near)), list(range(near, shards))]
        return lax.all_to_all(
            value, "emb", split_axis=0, concat_axis=0, axis_index_groups=groups, tiled=True
        )

    shape = jax.ShapeDtypeStruct
    held = functools.partial(pltpu.with_memory_space_constraint, memory_space=pltpu.HBM)
    mirrored = swap(table, across, 1)
    requests, codes, table = pl.pallas_call(
        functools.partial(request_kernel, slab),
        out_shape=(
            shape((near, 2 * reach), jnp.int32),
            shape((MB, count), jnp.int32),
            shape(table.shape, BF16),
        ),
        in_specs=[SMEM, VMEM, ANY],
        out_specs=(VMEM,) * 3,
        scratch_shapes=[pltpu.SemaphoreType.DMA],
        compiler_params=params(16),
        name="request",
    )(place, (owner[:, :, 0] * slab + row).reshape(MB, count), held(table))
    asked = exchange(requests)
    asked, *served = pl.pallas_call(
        near_kernel,
        out_shape=(shape(asked.shape, jnp.int32),) + (shape((reach, width), BF16),) * near,
        in_specs=[SMEM, VMEM, VMEM],
        out_specs=(VMEM,) * (1 + near),
        compiler_params=params(16),
        name="near",
    )(place, asked, table)
    served = pl.pallas_call(
        far_kernel,
        out_shape=(shape((2 * reach, width), BF16),) * near,
        in_specs=[VMEM] * (2 + near),
        out_specs=(VMEM,) * near,
        compiler_params=params(16),
        name="far",
    )(asked, mirrored, *served)
    order = ordered(near)
    fetched = [swap(served[step], peers, step) if step else served[0] for step in order]

    rounded, turned = pl.pallas_call(
        weight_kernel,
        out_shape=(shape(conv_weight.shape, BF16),) * 2,
        in_specs=[ANY],
        out_specs=(VMEM, VMEM),
        scratch_shapes=[
            pltpu.VMEM(conv_weight.shape, F32),
            pltpu.SemaphoreType.DMA((layers,)),
        ],
        compiler_params=params(16),
        name="weight",
    )(held(conv_weight))
    tokens = MB * count
    half = rows // 2
    padded = tokens + MB * PAD
    moved, keep, sent, block = pl.pallas_call(
        stack_kernel,
        out_shape=(
            shape((tokens, width), BF16),
            shape((half, width), BF16),
            shape((half + GROUP, width), BF16),
            shape((GROUP, width), BF16),
        ),
        in_specs=[SMEM, VMEM, VMEM, VMEM, ANY, ANY] + [VMEM] * near,
        out_specs=(VMEM,) * 4,
        scratch_shapes=[
            pltpu.VMEM((tokens, width), F32),
            pltpu.VMEM((2, padded, width), F32),
            pltpu.VMEM((layers, tokens, width), BF16),
            pltpu.VMEM((layers, tokens, width), F32),
            pltpu.VMEM((layers, tokens, 128), F32),
            pltpu.VMEM((layers, tokens, width), F32),
            pltpu.VMEM((2, padded, width), F32),
            pltpu.VMEM((2, tokens, taps), BF16),
            pltpu.VMEM((rows, width), F32),
            pltpu.VMEM((layers, width), F32),
            pltpu.VMEM((tokens, width), BF16),
            pltpu.SemaphoreType.DMA((2,)),
        ],
        compiler_params=params(36),
        name="stack",
    )(
        place, codes.reshape(tokens, 1), rounded, turned, held(gain),
        held(upstream.reshape(tokens, width)),
        *fetched,
    )

    chips = near // 2
    same, other = pl.pallas_call(
        place_kernel,
        out_shape=(shape((chips, 2 * reach, width), BF16),) * 2,
        in_specs=[VMEM, VMEM],
        out_specs=(VMEM, VMEM),
        compiler_params=params(24),
        name="place",
    )(codes, moved)
    other = swap(other, peers, 1)

    messages = [sent]
    share = slab // seqs
    for spot, bits in enumerate(stages[:-1]):
        arrived = [swap(message, bits, step + 1) for step, message in enumerate(messages)]
        parts = 2 ** len(stages[spot + 1])
        piece = keep.shape[0] // parts
        outs = (shape((piece, width), F32), shape((GROUP, width), BF16)) + (
            shape((piece + GROUP, width), BF16),
        ) * (parts - 1)
        rest = returned[1 : 1 + chips // 4] if spot == 1 else []
        keep, block, *messages = pl.pallas_call(
            functools.partial(fold_kernel, layers, len(arrived), parts, spot + 1),
            out_shape=outs,
            in_specs=[SMEM] + [VMEM] * (2 + len(arrived)) + [ANY] * len(rest),
            out_specs=(VMEM,) * len(outs),
            compiler_params=params(16),
            name=f"fold{spot}",
        )(place, keep, block, *arrived, *rest)
        if spot == 0:
            packed = pl.pallas_call(
                pack_kernel,
                out_shape=(shape((2, 2 * reach, width), BF16),) * chips,
                in_specs=[VMEM, VMEM, ANY],
                out_specs=(VMEM,) * chips,
                compiler_params=params(16),
                name="pack",
            )(same, other, block)
            returned = [
                swap(packed[step], peers[1:], step) if step else packed[0]
                for step in returning(chips)
            ]

    scale = float(seqs_dev * length * devices) ** (-0.5)
    arrived = [swap(message, stages[2], step + 1) for step, message in enumerate(messages)]
    keep, gain_grad = pl.pallas_call(
        functools.partial(last_kernel, layers, scale),
        out_shape=(shape(keep.shape, BF16), shape((layers, width), F32)),
        in_specs=[VMEM] * (2 + len(arrived)),
        out_specs=(VMEM,) * 2,
        compiler_params=params(16),
        name="last",
    )(keep, block, *arrived)
    near_share, far_share, *shares = pl.pallas_call(
        collect_kernel,
        out_shape=(shape((share, width), F32),) * 2
        + (shape((2 * share, width), BF16),) * (seqs - 1),
        in_specs=[SMEM, VMEM, ANY] + [VMEM] * chips,
        out_specs=(VMEM,) * (1 + seqs),
        scratch_shapes=[pltpu.VMEM((2, slab, width), F32)],
        compiler_params=params(24),
        name="collect",
    )(place, asked, keep, *returned)
    shares = [swap(value, group, step + 1) for step, value in enumerate(shares)]
    for bit in left:
        keep = (keep.astype(F32) + swap(keep, [bit], 1).astype(F32)).astype(BF16)
        gain_grad = gain_grad + swap(gain_grad, [bit], 1)

    line = [keep] + [swap(keep, stages[2], step) for step in range(1, 2 ** len(stages[2]))]
    keep = pl.pallas_call(
        line_kernel,
        out_shape=shape((half // 4, width), BF16),
        in_specs=[VMEM] * len(line),
        out_specs=VMEM,
        compiler_params=params(16),
        name="line",
    )(*line)
    near_share, far_share = pl.pallas_call(
        shares_kernel,
        out_shape=(shape((share, width), F32), shape((share, width), BF16)),
        in_specs=[ANY] + [VMEM] * (2 + len(shares)),
        out_specs=(VMEM,) * 2,
        compiler_params=params(16),
        name="shares",
    )(keep, near_share, far_share, *shares)
    far_share = swap(far_share, across, 1)
    square = [keep] + [swap(keep, stages[1], step) for step in range(1, 4)]
    other = [swap(value, stages[0], 1) for value in square]
    part = pl.pallas_call(
        share_kernel,
        out_shape=shape((share, width), BF16),
        in_specs=[VMEM, VMEM, ANY],
        out_specs=VMEM,
        compiler_params=params(16),
        name="share",
    )(near_share, far_share, square[3])
    pieces = [(side, outer) for side in range(2) for outer in range(4)]
    written = []
    for number, spots in enumerate((pieces[:5], pieces[5:])):
        written = pl.pallas_call(
            functools.partial(finish_kernel, 2 ** len(stages[2]), scale, spots),
            out_shape=(shape((rows, width), F32), shape((8, 128), F32))[: 1 + number],
            in_specs=[SMEM] + [VMEM] * len(spots) + [ANY] * number,
            out_specs=(ANY, VMEM)[: 1 + number],
            scratch_shapes=[
                pltpu.VMEM((len(spots), half // 4, width), F32),
                pltpu.SemaphoreType.DMA((len(spots),)),
            ],
            input_output_aliases={1 + len(spots): 0} if number else {},
            compiler_params=params(16),
            name=f"finish{number}",
        )(place, *[(square, other)[side][outer] for side, outer in spots], *written)
    weight_grad, mark = written
    table_grad = pl.pallas_call(
        table_kernel,
        out_shape=shape((slab, width), F32),
        in_specs=[SMEM, ANY] + [VMEM] * seqs,
        out_specs=VMEM,
        compiler_params=params(16),
        name="table",
    )(place, mark, part, *[swap(part, group, step) for step in range(1, seqs)])
    return (weight_grad.reshape(conv_weight.shape), gain_grad, table_grad)


def solution(mesh):
    in_specs = (
        P("emb", None),
        P(("emb", "seq"), None, None),
        P(("emb", "seq"), None),
        P(),
        P(),
        P(("emb", "seq"), None, None),
    )
    out_specs = (P(), P(), P("emb", None))
    return jax.shard_map(body, mesh=mesh, in_specs=in_specs, out_specs=out_specs, check_vma=False)
```
